256 devices in a mesh: gx: 16 (over z, core), gy: 16 (over y, x).
Axes of the slice: x: 4, y: 4, z: 8, core: 2. Of those that a mesh axis runs over, the one named last changes fastest.
Arguments:
- leaf_map: float32 [16, 16, 512, 512], P('gx', 'gy'), may hold values from -0.97 to 0.97, as said below
- source_trace: float32 [16, 16, 512], P('gx', 'gy'), may hold values from -6 to 6
- tile_class: int32 [16, 16, 16], P('gx', 'gy'), may hold values from 0 to 7
- absorb_table: float32 [8], replicated, may hold values from 0.2 to 2
Outputs:
- top_map: float32 [16, 16, 192, 1536], P('gx', 'gy')
- top_out: float32 [16, 16, 192], P('gx', 'gy')
The draws below stay inside these ranges and needn't reach their ends.
Inputs may be any that keep to these rules, and one draw needn't show every extreme that they name: `leaf_map`: each leaf map is a dense matrix whose largest singular value is at most 0.97.
All inputs are finite; a program needn't handle non-finite values.
Results may differ from the reference program's by a relative error of at most 0.000086.
Values sent between devices are 32-bit elements; how exact they have to be, the bound alone decides.
No kernel may reach another device: no remote copies, remote signals or barrier semaphores. Data moves between devices by JAX's collectives and lax.ppermute only.
A program may use at most 128 MiB of HBM per device.

```python
import math
import jax
import jax.numpy as jnp
from jax import lax

S = 128
SEG = 32
NCLASS = 8
BOXES_X = 16
BOXES_Y = 16
NSEG = 16
TOP = 1536
ROWS = 192


def orthogonal_draw(key, points):
    normal_block = jax.random.normal(key, (BOXES_X, BOXES_Y, points, points), jnp.float32)
    factor_q, factor_r = jnp.linalg.qr(normal_block)
    diagonal_r = jnp.diagonal(factor_r, axis1=-2, axis2=-1)
    signs = jnp.where(diagonal_r >= 0.0, 1.0, -1.0).astype(jnp.float32)
    return factor_q * signs[..., None, :]


def draw_leaf_map(key, part):
    points = 4 * S
    left_q = orthogonal_draw(jax.random.fold_in(key, 11), points)
    right_q = orthogonal_draw(jax.random.fold_in(key, 12), points)
    uniform_s = jax.random.uniform(jax.random.fold_in(key, 13), (BOXES_X, BOXES_Y, 1, points), jnp.float32, 0.0, 1.0)
    singular = 0.85 + 0.12 * uniform_s
    return jnp.matmul(left_q * singular, right_q, precision=lax.Precision.HIGHEST)


def touch_ends(drawn, rng, low, high):
    longest = drawn.shape.index(max(drawn.shape))
    spots = []
    for shift in (0, 1):
        where = [jax.random.randint(jax.random.fold_in(rng, axis), (), 0, length) for axis, length in enumerate(drawn.shape)]
        where[longest] = (where[longest] + shift) % drawn.shape[longest]
        spots.append(tuple(where))
    return drawn.at[spots[0]].set(low).at[spots[1]].set(high)


def block_levels(stream_key, dims, split, least, largest):
    loudness = 1.0
    for axis_at, shards_of in split:
        steps = jax.random.uniform(jax.random.fold_in(jax.random.fold_in(stream_key, 6), axis_at), (shards_of,), jnp.float32, least / len(split), largest / len(split))
        loudness = loudness * jnp.repeat(jnp.exp(steps), dims[axis_at] // shards_of).reshape((-1,) + (1,) * (len(dims) - 1 - axis_at))
    return loudness


def normal_values(stream_key, shape, width, most, shards=(), kind=jnp.bfloat16):
    values = width * jax.random.normal(stream_key, shape, jnp.float32)
    if shards:
        values = values * block_levels(stream_key, shape, shards, -0.22, 0.18)
    return jnp.clip(values, -most, most).astype(kind)


def setup_inputs(seed: int = 0) -> dict:
    arg_keys = jax.random.split(jax.random.key(seed), 5)
    return {
        "leaf_map": draw_leaf_map(jax.random.fold_in(arg_keys[4], 71), 0),
        "source_trace": normal_values(arg_keys[1], (BOXES_X, BOXES_Y, 4 * S), 1.0, 6.0, ((0, 16), (1, 16)), jnp.float32),
        "tile_class": touch_ends(jax.random.randint(arg_keys[2], (BOXES_X, BOXES_Y, NSEG), 0, NCLASS), jax.random.fold_in(arg_keys[2], 1), 0, NCLASS - 1).astype(jnp.int32),
        "absorb_table": jnp.clip(jnp.exp(jax.random.uniform(arg_keys[3], (NCLASS,), jnp.float32, math.log(0.2), math.log(2.0))), 0.2, 2.0),
    }


precise = lax.Precision.HIGHEST

def matmul_hi(left, right):
    return jnp.matmul(left, right, precision=precise)

def apply_vec(matrix, vector):
    return matmul_hi(matrix, vector[..., None])[..., 0]

def take_rows(matrix, spans):
    return jnp.concatenate([matrix[..., offset:offset + length, :] for offset, length in spans], axis=-2)

def take_cols(matrix, spans):
    return jnp.concatenate([matrix[..., offset:offset + length] for offset, length in spans], axis=-1)

def interface_solve(first_ie, first_ii, second_ie, second_ii, first_hi, second_hi):
    size_int = first_ii.shape[-1]
    coupling = jnp.eye(size_int, dtype=first_ii.dtype) - matmul_hi(first_ii, second_ii)
    right_side = jnp.concatenate([first_ie, -matmul_hi(first_ii, second_ie), (first_hi - apply_vec(first_ii, second_hi))[..., None]], axis=-1)
    coupling_t = jnp.swapaxes(coupling, -1, -2)
    factor = jnp.linalg.cholesky(matmul_hi(coupling_t, coupling))
    solved = jax.scipy.linalg.cho_solve((factor, True), matmul_hi(coupling_t, right_side))
    across = solved[..., :-1]
    across_h = solved[..., -1]
    beyond = jnp.concatenate([jnp.zeros_like(first_ie), second_ie], axis=-1) - matmul_hi(second_ii, across)
    beyond_h = second_hi - apply_vec(second_ii, across_h)
    return (across, across_h, beyond, beyond_h)

def merge_boxes(first_map, first_h, second_map, second_h, first_ext, first_int, second_ext, second_int):
    first_rows = take_rows(first_map, first_ext)
    first_irow = take_rows(first_map, first_int)
    second_rows = take_rows(second_map, second_ext)
    second_irow = take_rows(second_map, second_int)
    across, across_h, beyond, beyond_h = interface_solve(take_cols(first_irow, first_ext), take_cols(first_irow, first_int), take_cols(second_irow, second_ext), take_cols(second_irow, second_int), take_cols(first_h, first_int), take_cols(second_h, second_int))
    own_first = take_cols(first_rows, first_ext)
    link_first = take_cols(first_rows, first_int)
    own_second = take_cols(second_rows, second_ext)
    link_second = take_cols(second_rows, second_int)
    upper = jnp.concatenate([own_first, jnp.zeros(own_first.shape[:-1] + (own_second.shape[-1],), own_first.dtype)], axis=-1) - matmul_hi(link_first, beyond)
    lower = jnp.concatenate([jnp.zeros(own_second.shape[:-1] + (own_first.shape[-1],), own_second.dtype), own_second], axis=-1) - matmul_hi(link_second, across)
    merged = jnp.concatenate([upper, lower], axis=-2)
    merged_h = jnp.concatenate([take_cols(first_h, first_ext) - apply_vec(link_first, beyond_h), take_cols(second_h, second_ext) - apply_vec(link_second, across_h)], axis=-1)
    return (merged, merged_h)

def reorder(matrix, vector, order, unit):
    spans = [(position * unit, unit) for position in order]
    return (take_cols(take_rows(matrix, spans), spans), take_cols(vector, spans))

def reference(leaf_map, source_trace, tile_class, absorb_table):
    levels = absorb_table[tile_class]
    leaf_h = jnp.repeat(levels, SEG, axis=-1) * source_trace
    map1, h1 = merge_boxes(leaf_map[0::2], leaf_h[0::2], leaf_map[1::2], leaf_h[1::2], [(0, S), (2 * S, 2 * S)], [(S, S)], [(S, 3 * S)], [(0, S)])
    map1, h1 = reorder(map1, h1, [0, 3, 1, 4, 2, 5], S)
    map2, h2 = merge_boxes(map1[:, 0::2], h1[:, 0::2], map1[:, 1::2], h1[:, 1::2], [(0, 4 * S)], [(4 * S, 2 * S)], [(0, 2 * S), (4 * S, 2 * S)], [(2 * S, 2 * S)])
    map2, h2 = reorder(map2, h2, [0, 4, 1, 5, 2, 3, 6, 7], S)
    map3, h3 = merge_boxes(map2[0::2], h2[0::2], map2[1::2], h2[1::2], [(0, 2 * S), (4 * S, 4 * S)], [(2 * S, 2 * S)], [(2 * S, 6 * S)], [(0, 2 * S)])
    blocks = [h3[..., k * 2 * S:(k + 1) * 2 * S] for k in range(6)]
    zero_x = jnp.zeros_like(blocks[0][:1])
    from_west = jnp.concatenate([zero_x, blocks[3][:-1]], axis=0)
    from_east = jnp.concatenate([blocks[0][1:], zero_x], axis=0)
    north_edge = jnp.concatenate([blocks[2], blocks[5]], axis=-1)
    south_edge = jnp.concatenate([blocks[1], blocks[4]], axis=-1)
    zero_y = jnp.zeros_like(north_edge[:, :1])
    from_south = jnp.concatenate([zero_y, north_edge[:, :-1]], axis=1)
    from_north = jnp.concatenate([south_edge[:, 1:], zero_y], axis=1)
    incoming = -jnp.concatenate([from_west, from_south[..., :2 * S], from_north[..., :2 * S], from_east, from_south[..., 2 * S:], from_north[..., 2 * S:]], axis=-1)
    outgoing = apply_vec(map3, incoming) + h3
    tops_x = map3.shape[0]
    tops_y = map3.shape[1]
    scaled = map3 * math.sqrt(TOP)
    top_map = scaled.reshape(tops_x, tops_y, 4, 2, ROWS, TOP).transpose(0, 2, 1, 3, 4, 5).reshape(tops_x * 4, tops_y * 2, ROWS, TOP)
    top_out = outgoing.reshape(tops_x, tops_y, 4, 2, ROWS).transpose(0, 2, 1, 3, 4).reshape(tops_x * 4, tops_y * 2, ROWS)
    return (top_map, top_out)
```

```python
import math

import jax
import jax.numpy as jnp
from jax import lax
from jax.experimental import pallas as pl
from jax.experimental.pallas import tpu as pltpu
from jax.sharding import PartitionSpec as P

S = 128
f32 = jnp.float32
bf16 = jnp.bfloat16
HIGHEST = lax.Precision.HIGHEST


def roles():
    gx = lax.axis_index("gx")
    gy = lax.axis_index("gy")
    return gx % 2, gy % 2, (gx // 2) % 2


def at(offset, size, unit=S):
    return pl.ds(pl.multiple_of(offset * unit, unit), size)


def split(x):
    high = x.astype(bf16)
    return high, (x - high.astype(f32)).astype(bf16)


def mm(a, b):
    return jnp.dot(a, b, preferred_element_type=f32)


def dot3s(a, b):
    return mm(a[0], b[0]) + (mm(a[0], b[1]) + mm(a[1], b[0]))


def dot3(a, b):
    return dot3s(split(a), split(b))


def dot_full(a, b):
    return jnp.dot(a, b, precision=HIGHEST, preferred_element_type=f32)


def inverse(K):
    n = K.shape[0]
    rows = lax.broadcasted_iota(jnp.int32, (n, n), 0)
    cols = lax.broadcasted_iota(jnp.int32, (n, n), 1)
    eye = (rows == cols).astype(f32)
    ks = split(K)
    X = eye + K
    power = mm(ks[0], ks[0])
    steps = 6
    for j in range(1, steps + 1):
        pb = power.astype(bf16)
        if j < steps:
            both = mm(jnp.concatenate([X.astype(bf16), pb], 0), pb)
            X = X + both[:n]
            power = both[n:]
        else:
            X = X + mm(X.astype(bf16), pb)
    for _ in range(2):
        xs = split(X)
        residual = eye - X + dot3s(ks, xs)
        X = X + mm(xs[0], residual.astype(bf16))
    residual = eye - X + dot_full(K, X)
    return X + dot3(X, residual)


def as_columns(row):
    return jnp.broadcast_to(row, (S, S)).T


def as_rows(block):
    return block.T[:8]


def level1(own, oth, hown, hoth, m1, pii, xi, xe, r1, r2):
    c, s, r = roles()
    d = 1 - c
    P_ii = own[at(d, S), at(d, S)]
    Q_ii = oth[at(c, S), at(c, S)]
    P_ie = jnp.concatenate([own[at(d, S), at(c, S)], own[at(d, S), 2 * S :]], 1)
    Q_ie = jnp.concatenate([oth[at(c, S), at(d, S)], oth[at(c, S), 2 * S :]], 1)
    p_i = as_columns(hown[:, at(d, S)])
    q_i = as_columns(hoth[:, at(c, S)])
    Minv = inverse(dot_full(Q_ii, P_ii))
    U = dot3(Q_ii, jnp.concatenate([P_ie, p_i], 1))
    Z = jnp.concatenate([-U[:, : 3 * S], Q_ie, q_i - U[:, 3 * S :]], 1)
    T = dot3(Minv, Z)
    Tp = jnp.concatenate([P_ie, jnp.zeros((S, 3 * S), f32), p_i], 1) - dot3(P_ii, T)
    P_ei = jnp.concatenate([own[at(c, S), at(d, S)], own[2 * S :, at(d, S)]], 0)
    Q_ei = jnp.concatenate([oth[at(d, S), at(c, S)], oth[2 * S :, at(c, S)]], 0)
    DP = dot3(P_ei, T)
    DQ = dot3(Q_ei, Tp)
    for k in range(3):
        mine = slice(k * S, (k + 1) * S)
        row_own = at(c, S) if k == 0 else slice((k + 1) * S, (k + 2) * S)
        row_oth = at(d, S) if k == 0 else slice((k + 1) * S, (k + 2) * S)
        to_own = at(c + 2 * k, S)
        to_oth = at(d + 2 * k, S)
        for n in range(3):
            col_own = at(c, S) if n == 0 else slice((n + 1) * S, (n + 2) * S)
            col_oth = at(d, S) if n == 0 else slice((n + 1) * S, (n + 2) * S)
            n_own = slice(n * S, (n + 1) * S)
            n_oth = slice((n + 3) * S, (n + 4) * S)
            m1[to_own, at(c + 2 * n, S)] = own[row_own, col_own] - DP[mine, n_own]
            m1[to_own, at(d + 2 * n, S)] = -DP[mine, n_oth]
            m1[to_oth, at(d + 2 * n, S)] = oth[row_oth, col_oth] - DQ[mine, n_oth]
            m1[to_oth, at(c + 2 * n, S)] = -DQ[mine, n_own]
        h_own = hown[:, at(c, S)] if k == 0 else hown[:, (k + 1) * S : (k + 2) * S]
        h_oth = hoth[:, at(d, S)] if k == 0 else hoth[:, (k + 1) * S : (k + 2) * S]
        m1[to_own, 6 * S :] = as_columns(h_own) - DP[mine, 6 * S :]
        m1[to_oth, 6 * S :] = as_columns(h_oth) - DQ[mine, 6 * S :]
    row = at(2 * (2 - s) + c, S)
    pii[...] = m1[at(2 * (2 - s), 2 * S), at(2 * (2 - s), 2 * S)]
    xi[:S] = m1[row, at(2 * (2 - s), 2 * S)]
    xi[S:, :S] = as_rows(m1[row, 6 * S :])
    xi[S:, S:] = jnp.zeros((8, S), f32)
    xe[:, : 2 * S] = m1[row, : 2 * S]
    xe[:, 2 * S :] = m1[row, at(2 * (1 + s), 2 * S)]
    first = jnp.where(c == 0, jnp.where(s == 0, 4, 2 * r), 8)
    r1[...] = m1[at(first, S // 2, S // 2), :]
    r2[...] = m1[5 * S // 2 : 3 * S, :]


def level2_inverse(pii, xin, xic, minv, gii, qii):
    c, s, r = roles()
    qii[at(c, S), :] = xin[:S]
    qii[at(1 - c, S), :] = xic[:S]
    X = inverse(dot_full(qii[...], pii[...]))
    minv[...] = X
    gii[...] = dot3(X, qii[...])


def level2_interface(minv, gii, m1, xin, xic, xen, xec, t, y, yi, ye, qe):
    c, s, r = roles()
    o = 1 - s
    inner = at(2 * (2 - s), 2 * S)
    outer = at(2 * (1 + s), 2 * S)
    P_e = jnp.concatenate([m1[inner, : 2 * S], m1[inner, outer], m1[inner, 6 * S :]], 1)
    A = dot3(gii[...], P_e)
    qe[at(c, S), : 4 * S] = xen[...]
    qe[at(1 - c, S), : 4 * S] = xec[...]
    qe[at(c, S), 4 * S :] = as_columns(xin[S : S + 1, :S])
    qe[at(1 - c, S), 4 * S :] = as_columns(xic[S : S + 1, :S])
    B = dot3(minv[...], qe[...])
    t[:, at(s, S)] = -A[:, :S]
    t[:, at(2 + s, S)] = -A[:, S : 2 * S]
    t[:, at(4 + 2 * s, 2 * S)] = -A[:, 2 * S : 4 * S]
    t[:, at(o, S)] = B[:, :S]
    t[:, at(2 + o, S)] = B[:, S : 2 * S]
    t[:, at(4 + 2 * o, 2 * S)] = B[:, 2 * S : 4 * S]
    t[:, 8 * S :] = B[:, 4 * S :] - A[:, 4 * S :]
    row = at(1 - r, S)
    y[...] = -dot3(m1[row, inner], t[...])
    y[:, at(s, S)] += m1[row, :S]
    y[:, at(2 + s, S)] += m1[row, S : 2 * S]
    y[:, at(4 + 2 * s, 2 * S)] += m1[row, outer]
    y[:, 8 * S :] += m1[row, 6 * S :]
    half = at(c, S // 2, S // 2)
    yi[: S // 2] = y[half, at(2 * (1 - r), 2 * S)]
    yi[S // 2 :, :S] = as_rows(y[:, 8 * S :])
    yi[S // 2 :, S:] = jnp.zeros((8, S), f32)
    ye[:, : 2 * S] = y[half, at(2 * r, 2 * S)]
    ye[:, 2 * S :] = y[half, 4 * S : 8 * S]


def level2_rows(t, m1, r1n, r2n, rows, chip, work):
    c, s, r = roles()
    o = 1 - s
    H = S // 2
    inner = at(2 * (2 - s), 2 * S)
    outer = at(2 * (1 + s), 2 * S)
    m = 2 * c + s

    @pl.when(m == 0)
    def _():
        work[: 2 * H] = m1[at(2 * r, 2 * H, H), :]
        work[2 * H :] = r1n[...]

    @pl.when(m == 1)
    def _():
        work[:H] = m1[at(2 * r + 1, H, H), :]
        work[H : 2 * H] = r1n[...]
        work[2 * H :] = r2n[...]

    @pl.when(m == 2)
    def _():
        work[: 2 * H] = m1[6 * H : 8 * H, :]
        work[2 * H :] = r1n[...]

    @pl.when(m == 3)
    def _():
        work[...] = m1[9 * H : 12 * H, :]

    start = jnp.where(m == 1, H, jnp.where(m == 3, 3 * H, 2 * H))
    index = lax.broadcasted_iota(jnp.int32, (3 * H, 1), 0)
    got = index >= start
    V = dot3(work[:, outer], m1[inner, :])
    rows[:, : 7 * S] = V
    V_ii = rows[:, inner]
    V_pair = rows[:, outer]
    C = jnp.where(got, V_ii, -work[:, inner])
    D = dot3(C, t[...])
    own_side = jnp.where(got, -V[:, : 2 * S], work[:, : 2 * S])
    own_pair = jnp.where(got, -V_pair, work[:, outer])
    oth_side = jnp.where(got, work[:, : 2 * S], 0.0)
    oth_pair = jnp.where(got, work[:, inner], 0.0)
    data = work[:, 6 * S :] - jnp.where(got, V[:, 6 * S :], 0.0)
    rows[...] = D
    rows[:, at(s, S)] += own_side[:, :S]
    rows[:, at(2 + s, S)] += own_side[:, S:]
    rows[:, at(4 + 2 * s, 2 * S)] += own_pair
    rows[:, at(o, S)] += oth_side[:, :S]
    rows[:, at(2 + o, S)] += oth_side[:, S:]
    rows[:, at(4 + 2 * o, 2 * S)] += oth_pair
    rows[:, 8 * S :] += data
    P_ei = jnp.concatenate([m1[at(r, S), inner], m1[outer, inner]], 0)
    T_i = jnp.concatenate([t[:, at(2 * (1 - r), 2 * S)], t[:, 8 * S :]], 1)
    chip[...] = -dot3(P_ei, T_i)
    chip[:S, at(s, S)] += m1[at(r, S), at(1 - r, S)]
    chip[S:, at(s, S)] += m1[outer, at(1 - r, S)]
    chip[:S, 2 * S :] += m1[at(r, S), 6 * S :]
    chip[S:, 2 * S :] += m1[outer, 6 * S :]


def level3_inverse(y, yx, yz, yd, yxc, yzc, ydc, chip, minv, gii, th, hs, pii, qii, pq):
    c, s, r = roles()
    o = 1 - s
    d = 1 - c
    H = S // 2
    pii[at(s, S), :] = y[:, at(2 * (1 - r), 2 * S)]
    pii[at(2 * o + c, H, H), :] = yx[:H]
    pii[at(2 * o + d, H, H), :] = yxc[:H]
    qii[at(2 * s + c, H, H), :] = yz[:H]
    qii[at(2 * s + d, H, H), :] = yzc[:H]
    qii[at(2 * o + c, H, H), :] = yd[:H]
    qii[at(2 * o + d, H, H), :] = ydc[:H]
    pq[at(s, S), :S] = y[:, 8 * S :]
    pq[at(o, S), :S] = as_columns(yx[H : H + 1, :S])
    pq[at(s, S), S:] = as_columns(yz[H : H + 1, :S])
    pq[at(o, S), S:] = as_columns(yd[H : H + 1, :S])
    X = inverse(dot_full(qii[...], pii[...]))
    xs = split(X)
    minv[...] = X
    G = dot3s(xs, split(qii[...]))
    gii[...] = G
    tv = dot3s(xs, split(pq[:, S:])) - dot3(G, pq[:, :S])
    th[...] = tv
    h3 = chip[:, 2 * S :] - dot3(chip[:, : 2 * S], tv)
    hs[:, :S] = jnp.where(c == 0, as_rows(h3[:S]), as_rows(h3[S : 2 * S]))
    hs[:, S:] = as_rows(h3[2 * S :])


def level3_rows(minv, gii, th, y, yx, yz, yd, yxc, yzc, ydc, rows, top, h3, pe, qe):
    c, s, r = roles()
    o = 1 - s
    d = 1 - c
    H = S // 2
    pe[at(s, S), : 2 * S] = y[:, at(2 * r, 2 * S)]
    pe[at(s, S), 2 * S :] = y[:, 4 * S : 8 * S]
    pe[at(2 * o + c, H, H), :] = yx[...]
    pe[at(2 * o + d, H, H), :] = yxc[...]
    qe[at(2 * s + c, H, H), :] = yz[...]
    qe[at(2 * s + d, H, H), :] = yzc[...]
    qe[at(2 * o + c, H, H), :] = yd[...]
    qe[at(2 * o + d, H, H), :] = ydc[...]
    A = dot3(gii[...], pe[...])
    B = dot3(minv[...], qe[...])
    R_ei = split(rows[:, at(2 * (1 - r), 2 * S)])
    scale = math.sqrt(12 * S)
    R_ee = jnp.concatenate([rows[:, at(2 * r, 2 * S)], rows[:, 4 * S : 8 * S]], 1)
    top[:, at(6 * r, 6 * S)] = (R_ee + dot3s(R_ei, split(A))) * scale
    top[:, at(6 * (1 - r), 6 * S)] = dot3s(R_ei, split(B)) * (-scale)
    h3[...] = rows[:, 8 * S :] - dot3s(R_ei, split(th[...]))


def couple(top, h3, g0, gx, gz, gd, k0, kx, kz, kd, out, inc):
    c, s, r = roles()
    for mine, core, ss, rr in ((g0, k0, s, r), (gx, kx, 1 - s, r), (gz, kz, s, 1 - r), (gd, kd, 1 - s, 1 - r)):
        side = jnp.where(c == 0, mine[:, :S], core[:, :S])
        pair = jnp.where(c == 0, core[...], mine[...])
        inc[:, at(6 * rr + ss, S)] = side
        inc[:, at(6 * rr + 2 + 2 * ss, 2 * S)] = pair
    lane = lax.broadcasted_iota(jnp.int32, (h3.shape[0], S), 1)
    total = jnp.where(lane == 0, h3[...], 0.0)
    back = 1.0 / math.sqrt(12 * S)
    for k in range(12):
        total = total - top[:, k * S : (k + 1) * S] * (inc[0:1, k * S : (k + 1) * S] * back)
    lines = jnp.concatenate([total, jnp.zeros((2 * S - h3.shape[0], S), f32)], 0)
    flat = jnp.concatenate([lines[:S].T, lines[S:].T], 1)
    out[...] = jnp.sum(flat, 0, keepdims=True)[:, : h3.shape[0]]


def call(body, outs, scratch, args, flops):
    total = sum(a.size for a in args) + sum(math.prod(o) for o in outs)
    return pl.pallas_call(
        body,
        out_shape=[jax.ShapeDtypeStruct(o, f32) for o in outs],
        scratch_shapes=[pltpu.VMEM(x, f32) for x in scratch],
        compiler_params=pltpu.CompilerParams(vmem_limit_bytes=24 * 1024 * 1024),
        cost_estimate=pl.CostEstimate(flops=flops, bytes_accessed=4 * total, transcendentals=0),
        name=body.__name__,
    )(*args)


def send(value, to):
    nx, ny = lax.axis_size("gx"), lax.axis_size("gy")
    pairs = []
    for i in range(nx):
        for j in range(ny):
            goal = to(i, j)
            if goal is not None and 0 <= goal[0] < nx and 0 <= goal[1] < ny:
                pairs.append((i * ny + j, goal[0] * ny + goal[1]))
    return lax.ppermute(value, ("gx", "gy"), pairs)


def over_core(value):
    return send(value, lambda i, j: (i ^ 1, j))


def over_x(value):
    return send(value, lambda i, j: (i, j ^ 1))


def over_z(value):
    return send(value, lambda i, j: (i ^ 2, j))


def over_xz(value):
    return send(value, lambda i, j: (i ^ 2, j ^ 1))


def edge_target(i, j):
    if i % 2 == 0:
        return (i + 2, j) if (i // 2) % 2 else (i - 2, j)
    return (i, j + 1) if j % 2 else (i, j - 1)


def local(leaf_map, source_trace, tile_class, absorb_table):
    leaf = leaf_map[0, 0]
    classes = tile_class[0, 0]
    chosen = (classes[:, None] == jnp.arange(absorb_table.shape[0], dtype=jnp.int32)[None, :]).astype(f32)
    levels = jnp.sum(chosen * absorb_table[None, :], axis=1)
    seg = leaf.shape[0] // classes.shape[0]
    spread = jnp.broadcast_to(levels[:, None], (classes.shape[0], seg)).reshape(-1)
    hown = (spread * source_trace[0, 0])[None]

    oth = over_core(leaf)
    hoth = over_core(hown)
    m1, pii, xi, xe, r1, r2 = call(
        level1,
        [(6 * S, 7 * S), (2 * S, 2 * S), (S + 8, 2 * S), (S, 4 * S), (S // 2, 7 * S), (S // 2, 7 * S)],
        [],
        [leaf, oth, hown, hoth],
        3 * 2 * 768 * 128 * 896 * 2,
    )
    xin = over_x(xi)
    xic = over_core(xin)
    xen = over_x(xe)
    r1n = send(r1, lambda i, j: (i, j ^ 1) if (i % 2 == 0 or j % 2 == 1) else None)
    r2n = send(r2, lambda i, j: (i, j ^ 1) if (i % 2 == 0 and j % 2 == 0) else None)
    minv, gii = call(
        level2_inverse, [(2 * S, 2 * S)] * 2, [(2 * S, 2 * S)], [pii, xin, xic], 3 * 2 * 256**3 * 16
    )
    xec = over_core(xen)
    t, y, yi, ye = call(
        level2_interface,
        [(2 * S, 9 * S), (S, 9 * S), (S // 2 + 8, 2 * S), (S // 2, 6 * S)],
        [(2 * S, 5 * S)],
        [minv, gii, m1, xin, xic, xen, xec],
        3 * 2 * 256 * 256 * 1152 * 2,
    )
    yx, yz, yd = over_x(yi), over_z(yi), over_xz(yi)
    yxc, yzc, ydc = over_core(yx), over_core(yz), over_core(yd)
    ex, ez, ed = over_x(ye), over_z(ye), over_xz(ye)
    rows, chip = call(
        level2_rows,
        [(3 * S // 2, 9 * S), (3 * S, 3 * S)],
        [(3 * S // 2, 7 * S)],
        [t, m1, r1n, r2n],
        3 * 2 * 256 * 256 * 1152 * 2,
    )
    minv3, gii3, th, hs = call(
        level3_inverse,
        [(2 * S, 2 * S), (2 * S, 2 * S), (2 * S, S), (8, 2 * S)],
        [(2 * S, 2 * S)] * 3,
        [y, yx, yz, yd, yxc, yzc, ydc, chip],
        3 * 2 * 256**3 * 16,
    )
    exc, ezc, edc = over_core(ex), over_core(ez), over_core(ed)
    g0 = send(hs, edge_target)
    top, h3 = call(
        level3_rows,
        [(3 * S // 2, 12 * S), (3 * S // 2, S)],
        [(2 * S, 6 * S)] * 2,
        [minv3, gii3, th, y, ex, ez, ed, exc, ezc, edc, rows],
        3 * 2 * 256 * 256 * 1536 * 3,
    )
    gx, gz, gd = over_x(g0), over_z(g0), over_xz(g0)
    k0, kx, kz, kd = over_core(g0), over_core(gx), over_core(gz), over_core(gd)
    (out,) = call(
        couple, [(1, 3 * S // 2)], [(8, 12 * S)], [top, h3, g0, gx, gz, gd, k0, kx, kz, kd], 2 * 192 * 1536
    )
    return top[None, None], out[None]


def solution(mesh):
    return jax.shard_map(
        local,
        mesh=mesh,
        in_specs=(P("gx", "gy", None, None), P("gx", "gy", None), P("gx", "gy", None), P()),
        out_specs=(P("gx", "gy", None, None), P("gx", "gy", None)),
        check_vma=False,
    )
```

```python
import math

import jax
import jax.numpy as jnp
from jax import lax
from jax.experimental import pallas as pl
from jax.experimental.pallas import tpu as pltpu
from jax.sharding import PartitionSpec as P

S = 128
f32 = jnp.float32
bf16 = jnp.bfloat16
HIGHEST = lax.Precision.HIGHEST


def roles():
    gx = lax.axis_index("gx")
    gy = lax.axis_index("gy")
    return gx % 2, gy % 2, (gx // 2) % 2


def at(offset, size, unit=S):
    return pl.ds(pl.multiple_of(offset * unit, unit), size)


def split(x):
    high = x.astype(bf16)
    return high, (x - high.astype(f32)).astype(bf16)


def mm(a, b):
    return jnp.dot(a, b, preferred_element_type=f32)


def dot3s(a, b):
    return mm(a[0], b[0]) + (mm(a[0], b[1]) + mm(a[1], b[0]))


def dot3(a, b):
    return dot3s(split(a), split(b))


def dot_full(a, b):
    return jnp.dot(a, b, precision=HIGHEST, preferred_element_type=f32)


def inverse(K):
    n = K.shape[0]
    rows = lax.broadcasted_iota(jnp.int32, (n, n), 0)
    cols = lax.broadcasted_iota(jnp.int32, (n, n), 1)
    eye = (rows == cols).astype(f32)
    ks = split(K)
    X = eye + K
    power = mm(ks[0], ks[0])
    steps = 5
    for j in range(1, steps + 1):
        pb = power.astype(bf16)
        if j < steps:
            both = mm(jnp.concatenate([X.astype(bf16), pb], 0), pb)
            X = X + both[:n]
            power = both[n:]
        else:
            X = X + mm(X.astype(bf16), pb)
    for _ in range(2):
        xs = split(X)
        residual = eye - X + dot3s(ks, xs)
        X = X + mm(xs[0], residual.astype(bf16))
    residual = eye - X + dot_full(K, X)
    return X + dot3(X, residual)


def as_columns(row):
    return jnp.broadcast_to(row, (S, S)).T


def as_rows(block):
    return block.T[:8]


def bring(leaf, mark):
    mark[...] = leaf[:8, :S]


def level1_interface(own, oth, hown, hoth, mark, minv, pii, xi):
    c, s, r = roles()
    d = 1 - c
    e = 3 - s
    P_ii = own[at(d, S), at(d, S)]
    Q_ii = split(oth[at(c, S), at(c, S)])
    P_ie = own[at(d, S), at(e, S)]
    Q_ie = oth[at(c, S), at(e, S)]
    p_i = as_columns(hown[:, at(d, S)])
    q_i = as_columns(hoth[:, at(c, S)])
    X = inverse(dot_full(oth[at(c, S), at(c, S)], P_ii))
    minv[...] = X
    U = dot3s(Q_ii, split(jnp.concatenate([P_ie, p_i], 1)))
    T = split(dot3(X, jnp.concatenate([-U[:, :S], Q_ie, q_i - U[:, S:]], 1)))
    D = dot3s(split(own[at(e, S), at(d, S)]), T)
    Tp = jnp.concatenate([P_ie, jnp.zeros((S, S), f32)], 1) - dot3s(split(P_ii), (T[0][:, : 2 * S], T[1][:, : 2 * S]))
    DQ = dot3(oth[at(e, S), at(c, S)], Tp)
    pii[at(c, S), at(c, S)] = own[at(e, S), at(e, S)] - D[:, :S]
    pii[at(c, S), at(d, S)] = -D[:, S : 2 * S]
    pii[at(d, S), at(c, S)] = -DQ[:, :S]
    pii[at(d, S), at(d, S)] = oth[at(e, S), at(e, S)] - DQ[:, S:]
    xi[:S] = pii[at(c, S), :]
    xi[S:, :S] = as_rows(as_columns(hown[:, at(e, S)]) - D[:, 2 * S :])
    xi[S:, S:] = jnp.zeros((8, S), f32)


def level1_map(own, oth, hown, hoth, minv, m1, xe, xl):
    c, s, r = roles()
    d = 1 - c
    P_ii = own[at(d, S), at(d, S)]
    Q_ii = oth[at(c, S), at(c, S)]
    P_ie = jnp.concatenate([own[at(d, S), at(c, S)], own[at(d, S), 2 * S :]], 1)
    Q_ie = jnp.concatenate([oth[at(c, S), at(d, S)], oth[at(c, S), 2 * S :]], 1)
    p_i = as_columns(hown[:, at(d, S)])
    q_i = as_columns(hoth[:, at(c, S)])
    U = dot3(Q_ii, jnp.concatenate([P_ie, p_i], 1))
    Z = jnp.concatenate([-U[:, : 3 * S], Q_ie, q_i - U[:, 3 * S :]], 1)
    T = dot3(minv[...], Z)
    ts = split(T)
    Tp = jnp.concatenate([P_ie, jnp.zeros((S, 3 * S), f32), p_i], 1) - dot3s(split(P_ii), ts)
    P_ei = jnp.concatenate([own[at(c, S), at(d, S)], own[2 * S :, at(d, S)]], 0)
    Q_ei = jnp.concatenate([oth[at(d, S), at(c, S)], oth[2 * S :, at(c, S)]], 0)
    DP = dot3s(split(P_ei), ts)
    DQ = dot3(Q_ei, Tp)
    for k in range(3):
        mine = slice(k * S, (k + 1) * S)
        row_own = at(c, S) if k == 0 else slice((k + 1) * S, (k + 2) * S)
        row_oth = at(d, S) if k == 0 else slice((k + 1) * S, (k + 2) * S)
        to_own = at(c + 2 * k, S)
        to_oth = at(d + 2 * k, S)
        for n in range(3):
            col_own = at(c, S) if n == 0 else slice((n + 1) * S, (n + 2) * S)
            col_oth = at(d, S) if n == 0 else slice((n + 1) * S, (n + 2) * S)
            n_own = slice(n * S, (n + 1) * S)
            n_oth = slice((n + 3) * S, (n + 4) * S)
            m1[to_own, at(c + 2 * n, S)] = own[row_own, col_own] - DP[mine, n_own]
            m1[to_own, at(d + 2 * n, S)] = -DP[mine, n_oth]
            m1[to_oth, at(d + 2 * n, S)] = oth[row_oth, col_oth] - DQ[mine, n_oth]
            m1[to_oth, at(c + 2 * n, S)] = -DQ[mine, n_own]
        h_own = hown[:, at(c, S)] if k == 0 else hown[:, (k + 1) * S : (k + 2) * S]
        h_oth = hoth[:, at(d, S)] if k == 0 else hoth[:, (k + 1) * S : (k + 2) * S]
        m1[to_own, 6 * S :] = as_columns(h_own) - DP[mine, 6 * S :]
        m1[to_oth, 6 * S :] = as_columns(h_oth) - DQ[mine, 6 * S :]
    row = at(2 * (2 - s) + c, S)
    xe[:, : 2 * S] = m1[row, : 2 * S]
    xe[:, 2 * S :] = m1[row, at(2 * (1 + s), 2 * S)]
    xl[...] = m1[at(2 * (1 - r) + c, S // 2, S // 2), : 6 * S]


def pick(x, s, low, high):
    return jnp.where(s == 0, x[:, 2 * S * low : 2 * S * (low + 1)], x[:, 2 * S * high : 2 * S * (high + 1)])


def level2_inverse(pii, xin, xic, minv, gii, qii):
    c, s, r = roles()
    qii[at(c, S), :] = xin[:S]
    qii[at(1 - c, S), :] = xic[:S]
    X = inverse(dot_full(qii[...], pii[...]))
    minv[...] = X
    gii[...] = dot3(X, qii[...])


def level2_interface(minv, gii, m1, xin, xic, xen, xec, t, y, yi, yh, qe):
    c, s, r = roles()
    o = 1 - s
    inner = at(2 * (2 - s), 2 * S)
    outer = at(2 * (1 + s), 2 * S)
    P_e = jnp.concatenate([m1[inner, : 2 * S], m1[inner, outer], m1[inner, 6 * S :]], 1)
    A = dot3(gii[...], P_e)
    qe[at(c, S), : 4 * S] = xen[...]
    qe[at(1 - c, S), : 4 * S] = xec[...]
    qe[at(c, S), 4 * S :] = as_columns(xin[S : S + 1, :S])
    qe[at(1 - c, S), 4 * S :] = as_columns(xic[S : S + 1, :S])
    B = dot3(minv[...], qe[...])
    t[:, at(s, S)] = -A[:, :S]
    t[:, at(2 + s, S)] = -A[:, S : 2 * S]
    t[:, at(4 + 2 * s, 2 * S)] = -A[:, 2 * S : 4 * S]
    t[:, at(o, S)] = B[:, :S]
    t[:, at(2 + o, S)] = B[:, S : 2 * S]
    t[:, at(4 + 2 * o, 2 * S)] = B[:, 2 * S : 4 * S]
    t[:, 8 * S :] = B[:, 4 * S :] - A[:, 4 * S :]
    row = at(1 - r, S)
    y[...] = -dot3(m1[row, inner], t[...])
    y[:, at(s, S)] += m1[row, :S]
    y[:, at(2 + s, S)] += m1[row, S : 2 * S]
    y[:, at(4 + 2 * s, 2 * S)] += m1[row, outer]
    y[:, 8 * S :] += m1[row, 6 * S :]
    H = S // 2
    yi[:S] = y[:, at(2 * (1 - r), 2 * S)]
    yi[S:, :S] = as_rows(y[:, 8 * S :])
    yi[S:, S:] = jnp.zeros((8, S), f32)
    yh[:H] = yi[at(c, H, H), :]
    yh[H:] = yi[S:]


def level2_chip(t, m1, chip, rr):
    c, s, r = roles()
    inner = at(2 * (2 - s), 2 * S)
    outer = at(2 * (1 + s), 2 * S)
    P_ei = jnp.concatenate([m1[at(r, S), inner], m1[outer, inner]], 0)
    T_i = jnp.concatenate([t[:, at(2 * (1 - r), 2 * S)], t[:, 8 * S :]], 1)
    chip[...] = -dot3(P_ei, T_i)
    chip[:S, at(s, S)] += m1[at(r, S), at(1 - r, S)]
    chip[S:, at(s, S)] += m1[outer, at(1 - r, S)]
    chip[:S, 2 * S :] += m1[at(r, S), 6 * S :]
    chip[S:, 2 * S :] += m1[outer, 6 * S :]
    H = S // 2
    first = jnp.where(c == 0, jnp.where(s == 0, 4, 2 * r), jnp.where(s == 0, 5, 8))
    lines = at(first, H, H)
    rr[:H] = m1[lines, : 6 * S]
    rr[H:, :S] = as_rows(jnp.concatenate([m1[lines, 6 * S :]] * 2, 0))
    rr[H:, S:] = jnp.zeros((8, 5 * S), f32)


def level2_edge(t, m1, y, xln, xlc, be, yx, row):
    c, s, r = roles()
    o = 1 - s
    H = S // 2
    inner = at(2 * (2 - s), 2 * S)
    outer = at(2 * (1 + s), 2 * S)
    row[at(c, H, H), : 6 * S] = xln[...]
    row[at(1 - c, H, H), : 6 * S] = xlc[...]
    V = dot3(row[:, outer], m1[inner, : 6 * S])
    D = dot3(pick(V, s, 2, 1), jnp.concatenate([t[:, at(2 * r, 2 * S)], t[:, 4 * S : 8 * S]], 1))
    yx[...] = D
    yx[:, at(s, S)] -= jnp.where(r == 0, V[:, :S], V[:, S : 2 * S])
    yx[:, at(2 + 2 * s, 2 * S)] -= pick(V, s, 1, 2)
    yx[:, at(o, S)] += row[:, at(r, S)]
    yx[:, at(2 + 2 * o, 2 * S)] += row[:, inner]

    @pl.when(c == 0)
    def _():
        be[:, : 2 * S] = y[:, at(2 * r, 2 * S)]
        be[:, 2 * S :] = y[:, 4 * S : 8 * S]

    @pl.when(c == 1)
    def _():
        be[...] = yx[...]


def level2_rows(t, m1, rn, rc, rows, work):
    c, s, r = roles()
    o = 1 - s
    H = S // 2
    inner = at(2 * (2 - s), 2 * S)
    outer = at(2 * (1 + s), 2 * S)
    m = 2 * c + s

    @pl.when(m == 0)
    def _():
        work[: 2 * H] = m1[at(2 * r, 2 * H, H), :]

    @pl.when(m == 1)
    def _():
        work[:H] = m1[at(2 * r + 1, H, H), :]
        work[H : 2 * H, : 6 * S] = rn[:H]
        work[H : 2 * H, 6 * S :] = as_columns(rn[H : H + 1, :S])[:H]
        work[2 * H :, : 6 * S] = rc[:H]
        work[2 * H :, 6 * S :] = as_columns(rc[H : H + 1, :S])[:H]

    @pl.when(m == 2)
    def _():
        work[: 2 * H] = m1[6 * H : 8 * H, :]

    @pl.when((m == 0) | (m == 2))
    def _():
        work[2 * H :, : 6 * S] = rn[:H]
        work[2 * H :, 6 * S :] = as_columns(rn[H : H + 1, :S])[:H]

    @pl.when(m == 3)
    def _():
        work[...] = m1[9 * H : 12 * H, :]

    start = jnp.where(m == 1, H, jnp.where(m == 3, 3 * H, 2 * H))
    index = lax.broadcasted_iota(jnp.int32, (3 * H, 1), 0)
    got = index >= start
    V = dot3(work[:, outer], m1[inner, :])
    rows[:, : 7 * S] = V
    V_ii = rows[:, inner]
    V_pair = rows[:, outer]
    C = jnp.where(got, V_ii, -work[:, inner])
    D = dot3(C, t[...])
    own_side = jnp.where(got, -V[:, : 2 * S], work[:, : 2 * S])
    own_pair = jnp.where(got, -V_pair, work[:, outer])
    oth_side = jnp.where(got, work[:, : 2 * S], 0.0)
    oth_pair = jnp.where(got, work[:, inner], 0.0)
    data = work[:, 6 * S :] - jnp.where(got, V[:, 6 * S :], 0.0)
    rows[...] = D
    rows[:, at(s, S)] += own_side[:, :S]
    rows[:, at(2 + s, S)] += own_side[:, S:]
    rows[:, at(4 + 2 * s, 2 * S)] += own_pair
    rows[:, at(o, S)] += oth_side[:, :S]
    rows[:, at(2 + o, S)] += oth_side[:, S:]
    rows[:, at(4 + 2 * o, 2 * S)] += oth_pair
    rows[:, 8 * S :] += data


def level3_inverse(y, a1, k1, a2, k2, chip, minv, gii, th, hs, pii, qii, pq):
    c, s, r = roles()
    o = 1 - s
    d = 1 - c
    H = S // 2
    x = jnp.where(c == 0, a1[...], k1[...])
    z = jnp.where(c == 0, k1[...], a1[...])
    pii[at(s, S), :] = y[:, at(2 * (1 - r), 2 * S)]
    pii[at(o, S), :] = x[:S]
    qii[at(s, S), :] = z[:S]
    qii[at(2 * o + c, H, H), :] = a2[:H]
    qii[at(2 * o + d, H, H), :] = k2[:H]
    pq[at(s, S), :S] = y[:, 8 * S :]
    pq[at(o, S), :S] = as_columns(x[S : S + 1, :S])
    pq[at(s, S), S:] = as_columns(z[S : S + 1, :S])
    pq[at(o, S), S:] = as_columns(a2[H : H + 1, :S])
    X = inverse(dot_full(qii[...], pii[...]))
    xs = split(X)
    minv[...] = X
    G = dot3s(xs, split(qii[...]))
    gii[...] = G
    tv = dot3s(xs, split(pq[:, S:])) - dot3(G, pq[:, :S])
    th[...] = tv
    h3 = chip[:, 2 * S :] - dot3(chip[:, : 2 * S], tv)
    hs[:, :S] = jnp.where(c == 0, as_rows(h3[:S]), as_rows(h3[S : 2 * S]))
    hs[:, S:] = as_rows(h3[2 * S :])


def level3_rows(minv, gii, th, y, yx, be, kb, rows, top, raw, h3, pe, qe):
    c, s, r = roles()
    o = 1 - s
    pe[at(s, S), : 2 * S] = y[:, at(2 * r, 2 * S)]
    pe[at(s, S), 2 * S :] = y[:, 4 * S : 8 * S]
    pe[at(o, S), :] = yx[...]
    qe[at(s, S), :] = jnp.where(c == 0, be[...], kb[...])
    qe[at(o, S), :] = jnp.where(c == 0, kb[...], be[...])
    A = dot3(gii[...], pe[...])
    B = dot3(minv[...], qe[...])
    R_ei = split(rows[:, at(2 * (1 - r), 2 * S)])
    scale = math.sqrt(12 * S)
    R_ee = jnp.concatenate([rows[:, at(2 * r, 2 * S)], rows[:, 4 * S : 8 * S]], 1)
    own = R_ee + dot3s(R_ei, split(A))
    oth = -dot3s(R_ei, split(B))
    raw[:, at(6 * r, 6 * S)] = own
    raw[:, at(6 * (1 - r), 6 * S)] = oth
    top[...] = raw[...] * scale
    h3[...] = rows[:, 8 * S :] - dot3s(R_ei, split(th[...]))


def couple(raw, h3, g0, gx, gz, gd, k0, kx, kz, kd, out, inc):
    c, s, r = roles()
    box_x = lax.axis_index("gx") // 4
    box_y = lax.axis_index("gy") // 2
    last_x = lax.axis_size("gx") // 4 - 1
    last_y = lax.axis_size("gy") // 2 - 1
    edge_x = (box_x == 0) | (box_x == last_x)
    edge_y = (box_y == 0) | (box_y == last_y)
    at_x = jnp.where(box_x == 0, 0, 1)
    at_y = jnp.where(box_y == 0, 0, 1)
    for mine, core, ss, rr in ((g0, k0, s, r), (gx, kx, 1 - s, r), (gz, kz, s, 1 - r), (gd, kd, 1 - s, 1 - r)):
        side = jnp.where(c == 0, mine[:, :S], core[:, :S])
        pair = jnp.where(c == 0, core[...], mine[...])
        inc[:, at(6 * rr + ss, S)] = jnp.where(edge_x & (at_x == rr), 0.0, side)
        inc[:, at(6 * rr + 2 + 2 * ss, 2 * S)] = jnp.where(edge_y & (at_y == ss), 0.0, pair)
    lane = lax.broadcasted_iota(jnp.int32, (h3.shape[0], S), 1)
    total = jnp.where(lane == 0, h3[...], 0.0)
    for k in range(12):
        total = total - raw[:, k * S : (k + 1) * S] * inc[0:1, k * S : (k + 1) * S]
    lines = jnp.concatenate([total, jnp.zeros((2 * S - h3.shape[0], S), f32)], 0)
    flat = jnp.concatenate([lines[:S].T, lines[S:].T], 1)
    out[...] = jnp.sum(flat, 0, keepdims=True)[:, : h3.shape[0]]


def call(body, outs, scratch, args, us):
    whole = pl.BlockSpec(memory_space=pltpu.VMEM)
    return pl.pallas_call(
        body,
        out_shape=[jax.ShapeDtypeStruct(o, f32) for o in outs],
        in_specs=[whole] * len(args),
        out_specs=[whole] * len(outs),
        scratch_shapes=[pltpu.VMEM(x, f32) for x in scratch],
        compiler_params=pltpu.CompilerParams(vmem_limit_bytes=24 * 1024 * 1024),
        cost_estimate=pl.CostEstimate(flops=int(us * 1.15e9), bytes_accessed=0, transcendentals=0),
        name=body.__name__,
    )(*args)


def send(value, to):
    nx, ny = lax.axis_size("gx"), lax.axis_size("gy")
    pairs = []
    for i in range(nx):
        for j in range(ny):
            goal = to(i, j)
            if goal is not None and 0 <= goal[0] < nx and 0 <= goal[1] < ny:
                pairs.append((i * ny + j, goal[0] * ny + goal[1]))
    return lax.ppermute(value, ("gx", "gy"), pairs)


def after(value, *others):
    return lax.optimization_barrier((value, *others))[0]


def over_core(value):
    return send(value, lambda i, j: (i ^ 1, j))


def over_x(value):
    return send(value, lambda i, j: (i, j ^ 1))


def over_z(value):
    return send(value, lambda i, j: (i ^ 2, j))


def over_xz(value):
    return send(value, lambda i, j: (i ^ 2, j ^ 1))


def over_x_or_z(value):
    return send(value, lambda i, j: (i ^ 2, j) if i % 2 else (i, j ^ 1))


def over_edge(value):
    nx, ny = lax.axis_size("gx"), lax.axis_size("gy")

    def to(i, j):
        if i % 2 == 0:
            return ((i + 2) % nx if (i // 2) % 2 else (i - 2) % nx, j)
        return (i, (j + 1) % ny if j % 2 else (j - 1) % ny)

    return send(value, to)


def local(leaf_map, source_trace, tile_class, absorb_table):
    H = S // 2
    leaf = leaf_map[0, 0]
    oth = over_core(leaf)
    classes = tile_class[0, 0]
    chosen = (classes[:, None] == jnp.arange(absorb_table.shape[0], dtype=jnp.int32)[None, :]).astype(f32)
    levels = jnp.sum(chosen * absorb_table[None, :], axis=1)
    seg = leaf.shape[0] // classes.shape[0]
    spread = jnp.broadcast_to(levels[:, None], (classes.shape[0], seg)).reshape(-1)
    hown = (spread * source_trace[0, 0])[None]
    hoth = over_core(hown)
    (mark,) = call(bring, [(8, S)], [], [leaf], 1.0)
    minv1, pii, xi = call(
        level1_interface, [(S, S), (2 * S, 2 * S), (S + 8, 2 * S)], [], [leaf, oth, hown, hoth, mark], 2.5
    )
    xin = over_x(xi)
    m1, xe, xl = call(
        level1_map, [(6 * S, 7 * S), (S, 4 * S), (H, 6 * S)], [], [leaf, oth, hown, hoth, minv1], 2.0
    )
    xen = over_x(xe)
    xic = over_core(after(xin, xe))
    minv, gii = call(level2_inverse, [(2 * S, 2 * S)] * 2, [(2 * S, 2 * S)], [pii, xin, xic], 0.5)
    xec = over_core(after(xen, minv))
    xln = over_x(after(xl, xen, minv))
    t, y, yi, yh = call(
        level2_interface,
        [(2 * S, 9 * S), (S, 9 * S), (S + 8, 2 * S), (H + 8, 2 * S)],
        [(2 * S, 5 * S)],
        [minv, gii, m1, xin, xic, xen, xec],
        1.5,
    )
    a1, a2 = over_x_or_z(yi), over_xz(yh)
    chip, rr = call(level2_chip, [(3 * S, 3 * S), (H + 8, 6 * S)], [], [t, m1], 0.01)
    a1, a2, chip = lax.optimization_barrier((a1, a2, chip))
    k1, k2 = over_core(a1), over_core(a2)
    xlc = over_core(after(xln, chip))
    be, yx = call(level2_edge, [(S, 6 * S)] * 2, [(S, 6 * S)], [t, m1, y, xln, xlc], 0.01)
    bn = over_z(be)
    rn = over_x(after(rr, be))
    minv3, gii3, th, hs = call(
        level3_inverse,
        [(2 * S, 2 * S), (2 * S, 2 * S), (2 * S, S), (8, 2 * S)],
        [(2 * S, 2 * S)] * 3,
        [y, a1, k1, a2, k2, chip],
        20.0,
    )
    g0 = over_edge(hs)
    rc = over_core(after(rn, g0))
    kb = over_core(after(bn, g0))
    (rows,) = call(level2_rows, [(3 * H, 9 * S)], [(3 * H, 7 * S)], [t, m1, rn, rc], 1.5)
    gx, gz, gd = over_x(g0), over_z(g0), over_xz(g0)
    top, raw, h3 = call(
        level3_rows,
        [(3 * H, 12 * S), (3 * H, 12 * S), (3 * H, S)],
        [(2 * S, 6 * S)] * 2,
        [minv3, gii3, th, y, yx, bn, kb, rows],
        2.5,
    )
    g0, gx, gz, gd, h3 = lax.optimization_barrier((g0, gx, gz, gd, h3))
    k0, kx, kz, kd = over_core(g0), over_core(gx), over_core(gz), over_core(gd)
    (out,) = call(couple, [(1, 3 * H)], [(8, 12 * S)], [raw, h3, g0, gx, gz, gd, k0, kx, kz, kd], 0.7)
    return top[None, None], out[None]


def solution(mesh):
    return jax.shard_map(
        local,
        mesh=mesh,
        in_specs=(P("gx", "gy", None, None), P("gx", "gy", None), P("gx", "gy", None), P()),
        out_specs=(P("gx", "gy", None, None), P("gx", "gy", None)),
        check_vma=False,
    )
```

```python
import math

import jax
import jax.numpy as jnp
from jax import lax
from jax.experimental import pallas as pl
from jax.experimental.pallas import tpu as pltpu
from jax.sharding import PartitionSpec as P

S = 128
f32 = jnp.float32
bf16 = jnp.bfloat16
HIGHEST = lax.Precision.HIGHEST


def roles():
    gx = lax.axis_index("gx")
    gy = lax.axis_index("gy")
    return gx % 2, gy % 2, (gx // 2) % 2


def at(offset, size, unit=S):
    return pl.ds(pl.multiple_of(offset * unit, unit), size)


def split(x):
    high = x.astype(bf16)
    return high, (x - high.astype(f32)).astype(bf16)


def mm(a, b):
    return jnp.dot(a, b, preferred_element_type=f32)


def dot3s(a, b):
    return mm(a[0], b[0]) + (mm(a[0], b[1]) + mm(a[1], b[0]))


def dot3(a, b):
    return dot3s(split(a), split(b))


def dot_full(a, b):
    return jnp.dot(a, b, precision=HIGHEST, preferred_element_type=f32)


def inverse(K):
    n = K.shape[0]
    rows = lax.broadcasted_iota(jnp.int32, (n, n), 0)
    cols = lax.broadcasted_iota(jnp.int32, (n, n), 1)
    eye = (rows == cols).astype(f32)
    ks = split(K)
    X = eye + K
    power = mm(ks[0], ks[0])
    steps = 6
    for j in range(1, steps + 1):
        pb = power.astype(bf16)
        if j < steps:
            both = mm(jnp.concatenate([X.astype(bf16), pb], 0), pb)
            X = X + both[:n]
            power = both[n:]
        else:
            X = X + mm(X.astype(bf16), pb)
    xs = split(X)
    residual = eye - X + dot3s(ks, xs)
    X = X + mm(xs[0], residual.astype(bf16))
    residual = eye - X + dot_full(K, X)
    return X + dot3(X, residual)


def as_columns(row):
    return jnp.broadcast_to(row, (S, S)).T


def as_rows(block):
    return block.T[:8]


def bring(leaf, mark):
    mark[...] = leaf[:8, :S]


def level1_interface(own, oth, hown, hoth, mark, minv, pii, xi):
    c, s, r = roles()
    d = 1 - c
    e = 3 - s
    P_ii = own[at(d, S), at(d, S)]
    Q_ii = split(oth[at(c, S), at(c, S)])
    P_ie = own[at(d, S), at(e, S)]
    Q_ie = oth[at(c, S), at(e, S)]
    p_i = as_columns(hown[:, at(d, S)])
    q_i = as_columns(hoth[:, at(c, S)])
    X = inverse(dot_full(oth[at(c, S), at(c, S)], P_ii))
    minv[...] = X
    U = dot3s(Q_ii, split(jnp.concatenate([P_ie, p_i], 1)))
    T = split(dot3(X, jnp.concatenate([-U[:, :S], Q_ie, q_i - U[:, S:]], 1)))
    D = dot3s(split(own[at(e, S), at(d, S)]), T)
    Tp = jnp.concatenate([P_ie, jnp.zeros((S, S), f32)], 1) - dot3s(split(P_ii), (T[0][:, : 2 * S], T[1][:, : 2 * S]))
    DQ = dot3(oth[at(e, S), at(c, S)], Tp)
    pii[at(c, S), at(c, S)] = own[at(e, S), at(e, S)] - D[:, :S]
    pii[at(c, S), at(d, S)] = -D[:, S : 2 * S]
    pii[at(d, S), at(c, S)] = -DQ[:, :S]
    pii[at(d, S), at(d, S)] = oth[at(e, S), at(e, S)] - DQ[:, S:]
    xi[:S] = pii[at(c, S), :]
    xi[S:, :S] = as_rows(as_columns(hown[:, at(e, S)]) - D[:, 2 * S :])
    xi[S:, S:] = jnp.zeros((8, S), f32)


def level1_map(own, oth, hown, hoth, minv, m1, xe, xl):
    c, s, r = roles()
    d = 1 - c
    P_ii = own[at(d, S), at(d, S)]
    Q_ii = oth[at(c, S), at(c, S)]
    P_ie = jnp.concatenate([own[at(d, S), at(c, S)], own[at(d, S), 2 * S :]], 1)
    Q_ie = jnp.concatenate([oth[at(c, S), at(d, S)], oth[at(c, S), 2 * S :]], 1)
    p_i = as_columns(hown[:, at(d, S)])
    q_i = as_columns(hoth[:, at(c, S)])
    U = dot3(Q_ii, jnp.concatenate([P_ie, p_i], 1))
    Z = jnp.concatenate([-U[:, : 3 * S], Q_ie, q_i - U[:, 3 * S :]], 1)
    T = dot3(minv[...], Z)
    ts = split(T)
    Tp = jnp.concatenate([P_ie, jnp.zeros((S, 3 * S), f32), p_i], 1) - dot3s(split(P_ii), ts)
    P_ei = jnp.concatenate([own[at(c, S), at(d, S)], own[2 * S :, at(d, S)]], 0)
    Q_ei = jnp.concatenate([oth[at(d, S), at(c, S)], oth[2 * S :, at(c, S)]], 0)
    DP = dot3s(split(P_ei), ts)
    DQ = dot3(Q_ei, Tp)
    for k in range(3):
        mine = slice(k * S, (k + 1) * S)
        row_own = at(c, S) if k == 0 else slice((k + 1) * S, (k + 2) * S)
        row_oth = at(d, S) if k == 0 else slice((k + 1) * S, (k + 2) * S)
        to_own = at(c + 2 * k, S)
        to_oth = at(d + 2 * k, S)
        for n in range(3):
            col_own = at(c, S) if n == 0 else slice((n + 1) * S, (n + 2) * S)
            col_oth = at(d, S) if n == 0 else slice((n + 1) * S, (n + 2) * S)
            n_own = slice(n * S, (n + 1) * S)
            n_oth = slice((n + 3) * S, (n + 4) * S)
            m1[to_own, at(c + 2 * n, S)] = own[row_own, col_own] - DP[mine, n_own]
            m1[to_own, at(d + 2 * n, S)] = -DP[mine, n_oth]
            m1[to_oth, at(d + 2 * n, S)] = oth[row_oth, col_oth] - DQ[mine, n_oth]
            m1[to_oth, at(c + 2 * n, S)] = -DQ[mine, n_own]
        h_own = hown[:, at(c, S)] if k == 0 else hown[:, (k + 1) * S : (k + 2) * S]
        h_oth = hoth[:, at(d, S)] if k == 0 else hoth[:, (k + 1) * S : (k + 2) * S]
        m1[to_own, 6 * S :] = as_columns(h_own) - DP[mine, 6 * S :]
        m1[to_oth, 6 * S :] = as_columns(h_oth) - DQ[mine, 6 * S :]
    row = at(2 * (2 - s) + c, S)
    xe[:, : 2 * S] = m1[row, : 2 * S]
    xe[:, 2 * S :] = m1[row, at(2 * (1 + s), 2 * S)]
    xl[...] = m1[at(2 * (1 - r) + c, S // 2, S // 2), : 6 * S]


def pick(x, s, low, high):
    return jnp.where(s == 0, x[:, 2 * S * low : 2 * S * (low + 1)], x[:, 2 * S * high : 2 * S * (high + 1)])


def level2_inverse(pii, xin, xic, minv, gii, qii):
    c, s, r = roles()
    qii[at(c, S), :] = xin[:S]
    qii[at(1 - c, S), :] = xic[:S]
    X = inverse(dot_full(qii[...], pii[...]))
    minv[...] = X
    gii[...] = dot3(X, qii[...])


def level2_interface(minv, gii, m1, xin, xic, xen, xec, yi, yh, yd, qe):
    c, s, r = roles()
    d = 1 - c
    H = S // 2
    inner = at(2 * (2 - s), 2 * S)
    side = at(1 - r, S)
    A = dot3(gii[...], jnp.concatenate([m1[inner, side], m1[inner, 6 * S :]], 1))
    qe[at(c, S), :S] = xen[:, side]
    qe[at(d, S), :S] = xec[:, side]
    qe[at(c, S), S:] = as_columns(xin[S : S + 1, :S])
    qe[at(d, S), S:] = as_columns(xic[S : S + 1, :S])
    B = dot3(minv[...], qe[...])
    D = dot3(m1[side, inner], jnp.concatenate([A[:, :S], B[:, :S], B[:, S:] - A[:, S:]], 1))
    data = m1[side, 6 * S :] - D[:, 2 * S :]
    yd[...] = data
    yi[:S, at(s, S)] = m1[side, side] + D[:, :S]
    yi[:S, at(1 - s, S)] = -D[:, S : 2 * S]
    yi[S:, :S] = as_rows(data)
    yi[S:, S:] = jnp.zeros((8, S), f32)
    yh[:H] = yi[at(c, H, H), :]
    yh[H:] = yi[S:]


def level2_rest(minv, gii, m1, xin, xic, xen, xec, t, ye, chip, rr, qe):
    c, s, r = roles()
    o = 1 - s
    H = S // 2
    inner = at(2 * (2 - s), 2 * S)
    outer = at(2 * (1 + s), 2 * S)
    P_e = jnp.concatenate([m1[inner, : 2 * S], m1[inner, outer], m1[inner, 6 * S :]], 1)
    A = dot3(gii[...], P_e)
    qe[at(c, S), : 4 * S] = xen[...]
    qe[at(1 - c, S), : 4 * S] = xec[...]
    qe[at(c, S), 4 * S :] = as_columns(xin[S : S + 1, :S])
    qe[at(1 - c, S), 4 * S :] = as_columns(xic[S : S + 1, :S])
    B = dot3(minv[...], qe[...])
    t[:, at(s, S)] = -A[:, :S]
    t[:, at(2 + s, S)] = -A[:, S : 2 * S]
    t[:, at(4 + 2 * s, 2 * S)] = -A[:, 2 * S : 4 * S]
    t[:, at(o, S)] = B[:, :S]
    t[:, at(2 + o, S)] = B[:, S : 2 * S]
    t[:, at(4 + 2 * o, 2 * S)] = B[:, 2 * S : 4 * S]
    t[:, 8 * S :] = B[:, 4 * S :] - A[:, 4 * S :]
    row = at(1 - r, S)
    ye[...] = -dot3(m1[row, inner], jnp.concatenate([t[:, at(2 * r, 2 * S)], t[:, 4 * S : 8 * S]], 1))
    ye[:, at(s, S)] += m1[row, at(r, S)]
    ye[:, at(2 + 2 * s, 2 * S)] += m1[row, outer]
    P_ei = jnp.concatenate([m1[at(r, S), inner], m1[outer, inner]], 0)
    T_i = jnp.concatenate([t[:, at(2 * (1 - r), 2 * S)], t[:, 8 * S :]], 1)
    chip[...] = -dot3(P_ei, T_i)
    chip[:S, at(s, S)] += m1[at(r, S), at(1 - r, S)]
    chip[S:, at(s, S)] += m1[outer, at(1 - r, S)]
    chip[:S, 2 * S :] += m1[at(r, S), 6 * S :]
    chip[S:, 2 * S :] += m1[outer, 6 * S :]
    first = jnp.where(c == 0, jnp.where(s == 0, 4, 2 * r), jnp.where(s == 0, 5, 8))
    lines = at(first, H, H)
    rr[:H] = m1[lines, : 6 * S]
    rr[H:, :S] = as_rows(jnp.concatenate([m1[lines, 6 * S :]] * 2, 0))
    rr[H:, S:] = jnp.zeros((8, 5 * S), f32)


def level2_edge(t, m1, ye, xln, xlc, be, yx, row):
    c, s, r = roles()
    o = 1 - s
    H = S // 2
    inner = at(2 * (2 - s), 2 * S)
    outer = at(2 * (1 + s), 2 * S)
    row[at(c, H, H), : 6 * S] = xln[...]
    row[at(1 - c, H, H), : 6 * S] = xlc[...]
    V = dot3(row[:, outer], m1[inner, : 6 * S])
    D = dot3(pick(V, s, 2, 1), jnp.concatenate([t[:, at(2 * r, 2 * S)], t[:, 4 * S : 8 * S]], 1))
    yx[...] = D
    yx[:, at(s, S)] -= jnp.where(r == 0, V[:, :S], V[:, S : 2 * S])
    yx[:, at(2 + 2 * s, 2 * S)] -= pick(V, s, 1, 2)
    yx[:, at(o, S)] += row[:, at(r, S)]
    yx[:, at(2 + 2 * o, 2 * S)] += row[:, inner]

    @pl.when(c == 0)
    def _():
        be[...] = ye[...]

    @pl.when(c == 1)
    def _():
        be[...] = yx[...]


def level2_rows(t, m1, rn, rc, rows, work):
    c, s, r = roles()
    o = 1 - s
    H = S // 2
    inner = at(2 * (2 - s), 2 * S)
    outer = at(2 * (1 + s), 2 * S)
    m = 2 * c + s

    @pl.when(m == 0)
    def _():
        work[: 2 * H] = m1[at(2 * r, 2 * H, H), :]

    @pl.when(m == 1)
    def _():
        work[:H] = m1[at(2 * r + 1, H, H), :]
        work[H : 2 * H, : 6 * S] = rn[:H]
        work[H : 2 * H, 6 * S :] = as_columns(rn[H : H + 1, :S])[:H]
        work[2 * H :, : 6 * S] = rc[:H]
        work[2 * H :, 6 * S :] = as_columns(rc[H : H + 1, :S])[:H]

    @pl.when(m == 2)
    def _():
        work[: 2 * H] = m1[6 * H : 8 * H, :]

    @pl.when((m == 0) | (m == 2))
    def _():
        work[2 * H :, : 6 * S] = rn[:H]
        work[2 * H :, 6 * S :] = as_columns(rn[H : H + 1, :S])[:H]

    @pl.when(m == 3)
    def _():
        work[...] = m1[9 * H : 12 * H, :]

    start = jnp.where(m == 1, H, jnp.where(m == 3, 3 * H, 2 * H))
    index = lax.broadcasted_iota(jnp.int32, (3 * H, 1), 0)
    got = index >= start
    V = dot3(work[:, outer], m1[inner, :])
    rows[:, : 7 * S] = V
    V_ii = rows[:, inner]
    V_pair = rows[:, outer]
    C = jnp.where(got, V_ii, -work[:, inner])
    D = dot3(C, t[...])
    own_side = jnp.where(got, -V[:, : 2 * S], work[:, : 2 * S])
    own_pair = jnp.where(got, -V_pair, work[:, outer])
    oth_side = jnp.where(got, work[:, : 2 * S], 0.0)
    oth_pair = jnp.where(got, work[:, inner], 0.0)
    data = work[:, 6 * S :] - jnp.where(got, V[:, 6 * S :], 0.0)
    rows[...] = D
    rows[:, at(s, S)] += own_side[:, :S]
    rows[:, at(2 + s, S)] += own_side[:, S:]
    rows[:, at(4 + 2 * s, 2 * S)] += own_pair
    rows[:, at(o, S)] += oth_side[:, :S]
    rows[:, at(2 + o, S)] += oth_side[:, S:]
    rows[:, at(4 + 2 * o, 2 * S)] += oth_pair
    rows[:, 8 * S :] += data


def level3_inverse(yi, yd, a1, k1, a2, k2, chip, minv, gii, th, hs, pii, qii, pq):
    c, s, r = roles()
    o = 1 - s
    d = 1 - c
    H = S // 2
    x = jnp.where(c == 0, a1[...], k1[...])
    z = jnp.where(c == 0, k1[...], a1[...])
    pii[at(s, S), :] = yi[:S]
    pii[at(o, S), :] = x[:S]
    qii[at(s, S), :] = z[:S]
    qii[at(2 * o + c, H, H), :] = a2[:H]
    qii[at(2 * o + d, H, H), :] = k2[:H]
    pq[at(s, S), :S] = yd[...]
    pq[at(o, S), :S] = as_columns(x[S : S + 1, :S])
    pq[at(s, S), S:] = as_columns(z[S : S + 1, :S])
    pq[at(o, S), S:] = as_columns(a2[H : H + 1, :S])
    X = inverse(dot_full(qii[...], pii[...]))
    xs = split(X)
    minv[...] = X
    G = dot3s(xs, split(qii[...]))
    gii[...] = G
    tv = dot3s(xs, split(pq[:, S:])) - dot3(G, pq[:, :S])
    th[...] = tv
    h3 = chip[:, 2 * S :] - dot3(chip[:, : 2 * S], tv)
    hs[:, :S] = jnp.where(c == 0, as_rows(h3[:S]), as_rows(h3[S : 2 * S]))
    hs[:, S:] = as_rows(h3[2 * S :])


def level3_rows(minv, gii, th, ye, yx, be, kb, rows, top, raw, h3, pe, qe):
    c, s, r = roles()
    o = 1 - s
    pe[at(s, S), :] = ye[...]
    pe[at(o, S), :] = yx[...]
    qe[at(s, S), :] = jnp.where(c == 0, be[...], kb[...])
    qe[at(o, S), :] = jnp.where(c == 0, kb[...], be[...])
    A = dot3(gii[...], pe[...])
    B = dot3(minv[...], qe[...])
    R_ei = split(rows[:, at(2 * (1 - r), 2 * S)])
    scale = math.sqrt(12 * S)
    R_ee = jnp.concatenate([rows[:, at(2 * r, 2 * S)], rows[:, 4 * S : 8 * S]], 1)
    own = R_ee + dot3s(R_ei, split(A))
    oth = -dot3s(R_ei, split(B))
    raw[:, at(6 * r, 6 * S)] = own
    raw[:, at(6 * (1 - r), 6 * S)] = oth
    top[...] = raw[...] * scale
    h3[...] = rows[:, 8 * S :] - dot3s(R_ei, split(th[...]))


def couple(raw, h3, mine, core, out, inc):
    c, s, r = roles()
    box_x = lax.axis_index("gx") // 4
    box_y = lax.axis_index("gy") // 2
    last_x = lax.axis_size("gx") // 4 - 1
    last_y = lax.axis_size("gy") // 2 - 1
    edge_x = (box_x == 0) | (box_x == last_x)
    edge_y = (box_y == 0) | (box_y == last_y)
    at_x = jnp.where(box_x == 0, 0, 1)
    at_y = jnp.where(box_y == 0, 0, 1)
    for n, (ss, rr) in enumerate(((s, r), (1 - s, r), (s, 1 - r), (1 - s, 1 - r))):
        lines = slice(8 * n, 8 * n + 8)
        side = jnp.where(c == 0, mine[lines, :S], core[lines, :S])
        pair = jnp.where(c == 0, core[lines, :], mine[lines, :])
        inc[:, at(6 * rr + ss, S)] = jnp.where(edge_x & (at_x == rr), 0.0, side)
        inc[:, at(6 * rr + 2 + 2 * ss, 2 * S)] = jnp.where(edge_y & (at_y == ss), 0.0, pair)
    lane = lax.broadcasted_iota(jnp.int32, (h3.shape[0], S), 1)
    total = jnp.where(lane == 0, h3[...], 0.0)
    for k in range(12):
        total = total - raw[:, k * S : (k + 1) * S] * inc[0:1, k * S : (k + 1) * S]
    lines = jnp.concatenate([total, jnp.zeros((2 * S - h3.shape[0], S), f32)], 0)
    flat = jnp.concatenate([lines[:S].T, lines[S:].T], 1)
    out[...] = jnp.sum(flat, 0, keepdims=True)[:, : h3.shape[0]]


def call(body, outs, scratch, args, us):
    whole = pl.BlockSpec(memory_space=pltpu.VMEM)
    return pl.pallas_call(
        body,
        out_shape=[jax.ShapeDtypeStruct(o, f32) for o in outs],
        in_specs=[whole] * len(args),
        out_specs=[whole] * len(outs),
        scratch_shapes=[pltpu.VMEM(x, f32) for x in scratch],
        compiler_params=pltpu.CompilerParams(vmem_limit_bytes=24 * 1024 * 1024),
        cost_estimate=pl.CostEstimate(flops=int(us * 1.15e9), bytes_accessed=0, transcendentals=0),
        name=body.__name__,
    )(*args)


def send(value, to):
    nx, ny = lax.axis_size("gx"), lax.axis_size("gy")
    pairs = []
    for i in range(nx):
        for j in range(ny):
            goal = to(i, j)
            if goal is not None and 0 <= goal[0] < nx and 0 <= goal[1] < ny:
                pairs.append((i * ny + j, goal[0] * ny + goal[1]))
    return lax.ppermute(value, ("gx", "gy"), pairs)


def after(value, *others):
    return lax.optimization_barrier((value, *others))[0]


def over_core(value):
    return send(value, lambda i, j: (i ^ 1, j))


def over_x(value):
    return send(value, lambda i, j: (i, j ^ 1))


def over_z(value):
    return send(value, lambda i, j: (i ^ 2, j))


def over_xz(value):
    return send(value, lambda i, j: (i ^ 2, j ^ 1))


def over_x_or_z(value):
    return send(value, lambda i, j: (i ^ 2, j) if i % 2 else (i, j ^ 1))


def over_edge(value):
    nx, ny = lax.axis_size("gx"), lax.axis_size("gy")

    def to(i, j):
        if i % 2 == 0:
            return ((i + 2) % nx if (i // 2) % 2 else (i - 2) % nx, j)
        return (i, (j + 1) % ny if j % 2 else (j - 1) % ny)

    return send(value, to)


def local(leaf_map, source_trace, tile_class, absorb_table):
    H = S // 2
    leaf = leaf_map[0, 0]
    oth = over_core(leaf)
    classes = tile_class[0, 0]
    chosen = (classes[:, None] == jnp.arange(absorb_table.shape[0], dtype=jnp.int32)[None, :]).astype(f32)
    levels = jnp.sum(chosen * absorb_table[None, :], axis=1)
    seg = leaf.shape[0] // classes.shape[0]
    spread = jnp.broadcast_to(levels[:, None], (classes.shape[0], seg)).reshape(-1)
    hown = (spread * source_trace[0, 0])[None]
    hoth = over_core(hown)
    (mark,) = call(bring, [(8, S)], [], [leaf], 1.0)
    minv1, pii, xi = call(
        level1_interface, [(S, S), (2 * S, 2 * S), (S + 8, 2 * S)], [], [leaf, oth, hown, hoth, mark], 2.5
    )
    xin = over_x(xi)
    m1, xe, xl = call(
        level1_map, [(6 * S, 7 * S), (S, 4 * S), (H, 6 * S)], [], [leaf, oth, hown, hoth, minv1], 2.0
    )
    xen = over_x(xe)
    xic = over_core(after(xin, xe))
    minv, gii = call(level2_inverse, [(2 * S, 2 * S)] * 2, [(2 * S, 2 * S)], [pii, xin, xic], 0.5)
    xec = over_core(after(xen, minv))
    xln = over_x(after(xl, xen, minv))
    yi, yh, yd = call(
        level2_interface,
        [(S + 8, 2 * S), (H + 8, 2 * S), (S, S)],
        [(2 * S, 2 * S)],
        [minv, gii, m1, xin, xic, xen, xec],
        1.0,
    )
    a1, a2 = over_x_or_z(yi), over_xz(yh)
    t, ye, chip, rr = call(
        level2_rest,
        [(2 * S, 9 * S), (S, 6 * S), (3 * S, 3 * S), (H + 8, 6 * S)],
        [(2 * S, 5 * S)],
        [after(minv, yd), gii, m1, xin, xic, xen, xec],
        0.01,
    )
    a1, a2, chip = lax.optimization_barrier((a1, a2, chip))
    k1, k2 = over_core(a1), over_core(a2)
    xlc = over_core(after(xln, chip))
    be, yx = call(level2_edge, [(S, 6 * S)] * 2, [(S, 6 * S)], [t, m1, ye, xln, xlc], 0.01)
    bn = over_z(be)
    rn = over_x(after(rr, be))
    minv3, gii3, th, hs = call(
        level3_inverse,
        [(2 * S, 2 * S), (2 * S, 2 * S), (2 * S, S), (8, 2 * S)],
        [(2 * S, 2 * S)] * 3,
        [yi, yd, a1, k1, a2, k2, chip],
        20.0,
    )
    g0 = over_edge(hs)
    rc = over_core(after(rn, minv3))
    (rows,) = call(level2_rows, [(3 * H, 9 * S)], [(3 * H, 7 * S)], [t, m1, rn, rc], 1.5)
    bn, g0, rows = lax.optimization_barrier((bn, g0, rows))
    kb = over_core(bn)
    gx, gz, gd = over_x(g0), over_z(g0), over_xz(g0)
    top, raw, h3 = call(
        level3_rows,
        [(3 * H, 12 * S), (3 * H, 12 * S), (3 * H, S)],
        [(2 * S, 6 * S)] * 2,
        [minv3, gii3, th, ye, yx, bn, kb, rows],
        2.5,
    )
    g0, gx, gz, gd, h3 = lax.optimization_barrier((g0, gx, gz, gd, h3))
    edges = jnp.concatenate([g0, gx, gz, gd], 0)
    (out,) = call(couple, [(1, 3 * H)], [(8, 12 * S)], [raw, h3, edges, over_core(edges)], 0.7)
    return top[None, None], out[None]


def solution(mesh):
    return jax.shard_map(
        local,
        mesh=mesh,
        in_specs=(P("gx", "gy", None, None), P("gx", "gy", None), P("gx", "gy", None), P()),
        out_specs=(P("gx", "gy", None, None), P("gx", "gy", None)),
        check_vma=False,
    )
```

```python
import math

import jax
import jax.numpy as jnp
from jax import lax
from jax.experimental import pallas as pl
from jax.experimental.pallas import tpu as pltpu
from jax.sharding import PartitionSpec as P

S = 128
f32 = jnp.float32
bf16 = jnp.bfloat16
HIGHEST = lax.Precision.HIGHEST


def roles():
    gx = lax.axis_index("gx")
    gy = lax.axis_index("gy")
    return gx % 2, gy % 2, (gx // 2) % 2


def at(offset, size, unit=S):
    return pl.ds(pl.multiple_of(offset * unit, unit), size)


def split(x):
    high = x.astype(bf16)
    return high, (x - high.astype(f32)).astype(bf16)


def mm(a, b):
    return jnp.dot(a, b, preferred_element_type=f32)


def dot3s(a, b):
    return mm(a[0], b[0]) + (mm(a[0], b[1]) + mm(a[1], b[0]))


def dot3(a, b):
    return dot3s(split(a), split(b))


def dot_full(a, b):
    return jnp.dot(a, b, precision=HIGHEST, preferred_element_type=f32)


def inverse(K):
    n = K.shape[0]
    rows = lax.broadcasted_iota(jnp.int32, (n, n), 0)
    cols = lax.broadcasted_iota(jnp.int32, (n, n), 1)
    eye = (rows == cols).astype(f32)
    ks = split(K)
    X = eye + K
    power = mm(ks[0], ks[0])
    steps = 6
    for j in range(1, steps + 1):
        pb = power.astype(bf16)
        if j < steps:
            both = mm(jnp.concatenate([X.astype(bf16), pb], 0), pb)
            X = X + both[:n]
            power = both[n:]
        else:
            X = X + mm(X.astype(bf16), pb)
    xs = split(X)
    residual = eye - X + dot3s(ks, xs)
    X = X + mm(xs[0], residual.astype(bf16))
    residual = eye - X + dot_full(K, X)
    return X + dot3(X, residual)


def as_columns(row):
    return jnp.broadcast_to(row, (S, S)).T


def as_rows(block):
    return block.T[:8]


def bring(leaf, mark):
    mark[...] = leaf[:8, :S]


def level1_interface(own, oth, hown, hoth, mark, minv, pii, xi):
    c, s, r = roles()
    d = 1 - c
    e = 3 - s
    P_ii = own[at(d, S), at(d, S)]
    Q_ii = split(oth[at(c, S), at(c, S)])
    P_ie = own[at(d, S), at(e, S)]
    Q_ie = oth[at(c, S), at(e, S)]
    p_i = as_columns(hown[:, at(d, S)])
    q_i = as_columns(hoth[:, at(c, S)])
    X = inverse(dot_full(oth[at(c, S), at(c, S)], P_ii))
    minv[...] = X
    U = dot3s(Q_ii, split(jnp.concatenate([P_ie, p_i], 1)))
    T = split(dot3(X, jnp.concatenate([-U[:, :S], Q_ie, q_i - U[:, S:]], 1)))
    D = dot3s(split(own[at(e, S), at(d, S)]), T)
    Tp = jnp.concatenate([P_ie, jnp.zeros((S, S), f32)], 1) - dot3s(split(P_ii), (T[0][:, : 2 * S], T[1][:, : 2 * S]))
    DQ = dot3(oth[at(e, S), at(c, S)], Tp)
    pii[at(c, S), at(c, S)] = own[at(e, S), at(e, S)] - D[:, :S]
    pii[at(c, S), at(d, S)] = -D[:, S : 2 * S]
    pii[at(d, S), at(c, S)] = -DQ[:, :S]
    pii[at(d, S), at(d, S)] = oth[at(e, S), at(e, S)] - DQ[:, S:]
    xi[:S] = pii[at(c, S), :]
    xi[S:, :S] = as_rows(as_columns(hown[:, at(e, S)]) - D[:, 2 * S :])
    xi[S:, S:] = jnp.zeros((8, S), f32)


def level1_map(own, oth, hown, hoth, minv, m1, xe, xl):
    c, s, r = roles()
    d = 1 - c
    P_ii = own[at(d, S), at(d, S)]
    Q_ii = oth[at(c, S), at(c, S)]
    P_ie = jnp.concatenate([own[at(d, S), at(c, S)], own[at(d, S), 2 * S :]], 1)
    Q_ie = jnp.concatenate([oth[at(c, S), at(d, S)], oth[at(c, S), 2 * S :]], 1)
    p_i = as_columns(hown[:, at(d, S)])
    q_i = as_columns(hoth[:, at(c, S)])
    U = dot3(Q_ii, jnp.concatenate([P_ie, p_i], 1))
    Z = jnp.concatenate([-U[:, : 3 * S], Q_ie, q_i - U[:, 3 * S :]], 1)
    T = dot3(minv[...], Z)
    ts = split(T)
    Tp = jnp.concatenate([P_ie, jnp.zeros((S, 3 * S), f32), p_i], 1) - dot3s(split(P_ii), ts)
    P_ei = jnp.concatenate([own[at(c, S), at(d, S)], own[2 * S :, at(d, S)]], 0)
    Q_ei = jnp.concatenate([oth[at(d, S), at(c, S)], oth[2 * S :, at(c, S)]], 0)
    DP = dot3s(split(P_ei), ts)
    DQ = dot3(Q_ei, Tp)
    for k in range(3):
        mine = slice(k * S, (k + 1) * S)
        row_own = at(c, S) if k == 0 else slice((k + 1) * S, (k + 2) * S)
        row_oth = at(d, S) if k == 0 else slice((k + 1) * S, (k + 2) * S)
        to_own = at(c + 2 * k, S)
        to_oth = at(d + 2 * k, S)
        for n in range(3):
            col_own = at(c, S) if n == 0 else slice((n + 1) * S, (n + 2) * S)
            col_oth = at(d, S) if n == 0 else slice((n + 1) * S, (n + 2) * S)
            n_own = slice(n * S, (n + 1) * S)
            n_oth = slice((n + 3) * S, (n + 4) * S)
            m1[to_own, at(c + 2 * n, S)] = own[row_own, col_own] - DP[mine, n_own]
            m1[to_own, at(d + 2 * n, S)] = -DP[mine, n_oth]
            m1[to_oth, at(d + 2 * n, S)] = oth[row_oth, col_oth] - DQ[mine, n_oth]
            m1[to_oth, at(c + 2 * n, S)] = -DQ[mine, n_own]
        h_own = hown[:, at(c, S)] if k == 0 else hown[:, (k + 1) * S : (k + 2) * S]
        h_oth = hoth[:, at(d, S)] if k == 0 else hoth[:, (k + 1) * S : (k + 2) * S]
        m1[to_own, 6 * S :] = as_columns(h_own) - DP[mine, 6 * S :]
        m1[to_oth, 6 * S :] = as_columns(h_oth) - DQ[mine, 6 * S :]
    row = at(2 * (2 - s) + c, S)
    xe[:, : 2 * S] = m1[row, : 2 * S]
    xe[:, 2 * S :] = m1[row, at(2 * (1 + s), 2 * S)]
    half = at(2 * (1 - r) + c, S // 2, S // 2)
    xl[:, :S] = m1[half, at(r, S)]
    xl[:, S:] = m1[half, 2 * S : 6 * S]


def pick(x, s, low, high):
    return jnp.where(s == 0, x[:, 2 * S * low : 2 * S * (low + 1)], x[:, 2 * S * high : 2 * S * (high + 1)])


def level2_inverse(pii, xin, xic, minv, gii, qii):
    c, s, r = roles()
    qii[at(c, S), :] = xin[:S]
    qii[at(1 - c, S), :] = xic[:S]
    X = inverse(dot_full(qii[...], pii[...]))
    minv[...] = X
    gii[...] = dot3(X, qii[...])


def level2_interface(minv, gii, m1, xin, xic, xen, xec, yi, yh, yd, qe):
    c, s, r = roles()
    d = 1 - c
    H = S // 2
    inner = at(2 * (2 - s), 2 * S)
    side = at(1 - r, S)
    A = dot3(gii[...], jnp.concatenate([m1[inner, side], m1[inner, 6 * S :]], 1))
    qe[at(c, S), :S] = xen[:, side]
    qe[at(d, S), :S] = xec[:, side]
    qe[at(c, S), S:] = as_columns(xin[S : S + 1, :S])
    qe[at(d, S), S:] = as_columns(xic[S : S + 1, :S])
    B = dot3(minv[...], qe[...])
    D = dot3(m1[side, inner], jnp.concatenate([A[:, :S], B[:, :S], B[:, S:] - A[:, S:]], 1))
    data = m1[side, 6 * S :] - D[:, 2 * S :]
    yd[...] = data
    yi[:S, at(s, S)] = m1[side, side] + D[:, :S]
    yi[:S, at(1 - s, S)] = -D[:, S : 2 * S]
    yi[S:, :S] = as_rows(data)
    yi[S:, S:] = jnp.zeros((8, S), f32)
    yh[:H] = yi[at(c, H, H), :]
    yh[H:] = yi[S:]


def level2_rest(minv, gii, m1, xin, xic, xen, xec, t, ye, chip, rr, qe):
    c, s, r = roles()
    o = 1 - s
    H = S // 2
    inner = at(2 * (2 - s), 2 * S)
    outer = at(2 * (1 + s), 2 * S)
    P_e = jnp.concatenate([m1[inner, : 2 * S], m1[inner, outer], m1[inner, 6 * S :]], 1)
    A = dot3(gii[...], P_e)
    qe[at(c, S), : 4 * S] = xen[...]
    qe[at(1 - c, S), : 4 * S] = xec[...]
    qe[at(c, S), 4 * S :] = as_columns(xin[S : S + 1, :S])
    qe[at(1 - c, S), 4 * S :] = as_columns(xic[S : S + 1, :S])
    B = dot3(minv[...], qe[...])
    t[:, at(s, S)] = -A[:, :S]
    t[:, at(2 + s, S)] = -A[:, S : 2 * S]
    t[:, at(4 + 2 * s, 2 * S)] = -A[:, 2 * S : 4 * S]
    t[:, at(o, S)] = B[:, :S]
    t[:, at(2 + o, S)] = B[:, S : 2 * S]
    t[:, at(4 + 2 * o, 2 * S)] = B[:, 2 * S : 4 * S]
    t[:, 8 * S :] = B[:, 4 * S :] - A[:, 4 * S :]
    row = at(1 - r, S)
    ye[...] = -dot3(m1[row, inner], jnp.concatenate([t[:, at(2 * r, 2 * S)], t[:, 4 * S : 8 * S]], 1))
    ye[:, at(s, S)] += m1[row, at(r, S)]
    ye[:, at(2 + 2 * s, 2 * S)] += m1[row, outer]
    P_ei = jnp.concatenate([m1[at(r, S), inner], m1[outer, inner]], 0)
    T_i = jnp.concatenate([t[:, at(2 * (1 - r), 2 * S)], t[:, 8 * S :]], 1)
    chip[...] = -dot3(P_ei, T_i)
    chip[:S, at(s, S)] += m1[at(r, S), at(1 - r, S)]
    chip[S:, at(s, S)] += m1[outer, at(1 - r, S)]
    chip[:S, 2 * S :] += m1[at(r, S), 6 * S :]
    chip[S:, 2 * S :] += m1[outer, 6 * S :]
    first = jnp.where(c == 0, jnp.where(s == 0, 4, 2 * r), jnp.where(s == 0, 5, 8))
    lines = at(first, H, H)
    rr[:H] = m1[lines, : 6 * S]
    rr[H:, :S] = as_rows(jnp.concatenate([m1[lines, 6 * S :]] * 2, 0))
    rr[H:, S:] = jnp.zeros((8, 5 * S), f32)


def level2_edge(t, m1, ye, xln, be, yx):
    c, s, r = roles()
    o = 1 - s
    H = S // 2
    inner = at(2 * (2 - s), 2 * S)
    link = pick(xln[:, S:], s, 0, 1)
    V = dot3(link, m1[inner, : 6 * S])
    D = dot3(pick(V, s, 2, 1), jnp.concatenate([t[:, at(2 * r, 2 * S)], t[:, 4 * S : 8 * S]], 1))
    yx[...] = D
    yx[:, at(s, S)] -= jnp.where(r == 0, V[:, :S], V[:, S : 2 * S])
    yx[:, at(2 + 2 * s, 2 * S)] -= pick(V, s, 1, 2)
    yx[:, at(o, S)] += xln[:, :S]
    yx[:, at(2 + 2 * o, 2 * S)] += pick(xln[:, S:], s, 1, 0)
    be[:H] = ye[at(c, H, H), :]
    be[H:] = yx[...]


def level2_rows(t, m1, rn, rc, rows, work):
    c, s, r = roles()
    o = 1 - s
    H = S // 2
    inner = at(2 * (2 - s), 2 * S)
    outer = at(2 * (1 + s), 2 * S)
    m = 2 * c + s

    @pl.when(m == 0)
    def _():
        work[: 2 * H] = m1[at(2 * r, 2 * H, H), :]

    @pl.when(m == 1)
    def _():
        work[:H] = m1[at(2 * r + 1, H, H), :]
        work[H : 2 * H, : 6 * S] = rn[:H]
        work[H : 2 * H, 6 * S :] = as_columns(rn[H : H + 1, :S])[:H]
        work[2 * H :, : 6 * S] = rc[:H]
        work[2 * H :, 6 * S :] = as_columns(rc[H : H + 1, :S])[:H]

    @pl.when(m == 2)
    def _():
        work[: 2 * H] = m1[6 * H : 8 * H, :]

    @pl.when((m == 0) | (m == 2))
    def _():
        work[2 * H :, : 6 * S] = rn[:H]
        work[2 * H :, 6 * S :] = as_columns(rn[H : H + 1, :S])[:H]

    @pl.when(m == 3)
    def _():
        work[...] = m1[9 * H : 12 * H, :]

    start = jnp.where(m == 1, H, jnp.where(m == 3, 3 * H, 2 * H))
    index = lax.broadcasted_iota(jnp.int32, (3 * H, 1), 0)
    got = index >= start
    V = dot3(work[:, outer], m1[inner, :])
    rows[:, : 7 * S] = V
    V_ii = rows[:, inner]
    V_pair = rows[:, outer]
    C = jnp.where(got, V_ii, -work[:, inner])
    D = dot3(C, t[...])
    own_side = jnp.where(got, -V[:, : 2 * S], work[:, : 2 * S])
    own_pair = jnp.where(got, -V_pair, work[:, outer])
    oth_side = jnp.where(got, work[:, : 2 * S], 0.0)
    oth_pair = jnp.where(got, work[:, inner], 0.0)
    data = work[:, 6 * S :] - jnp.where(got, V[:, 6 * S :], 0.0)
    rows[...] = D
    rows[:, at(s, S)] += own_side[:, :S]
    rows[:, at(2 + s, S)] += own_side[:, S:]
    rows[:, at(4 + 2 * s, 2 * S)] += own_pair
    rows[:, at(o, S)] += oth_side[:, :S]
    rows[:, at(2 + o, S)] += oth_side[:, S:]
    rows[:, at(4 + 2 * o, 2 * S)] += oth_pair
    rows[:, 8 * S :] += data


def level3_inverse(yi, yd, a1, k1, a2, k2, chip, minv, gii, th, hs, pii, qii, pq):
    c, s, r = roles()
    o = 1 - s
    d = 1 - c
    H = S // 2
    x = jnp.where(c == 0, a1[...], k1[...])
    z = jnp.where(c == 0, k1[...], a1[...])
    pii[at(s, S), :] = yi[:S]
    pii[at(o, S), :] = x[:S]
    qii[at(s, S), :] = z[:S]
    qii[at(2 * o + c, H, H), :] = a2[:H]
    qii[at(2 * o + d, H, H), :] = k2[:H]
    pq[at(s, S), :S] = yd[...]
    pq[at(o, S), :S] = as_columns(x[S : S + 1, :S])
    pq[at(s, S), S:] = as_columns(z[S : S + 1, :S])
    pq[at(o, S), S:] = as_columns(a2[H : H + 1, :S])
    X = inverse(dot_full(qii[...], pii[...]))
    xs = split(X)
    minv[...] = X
    G = dot3s(xs, split(qii[...]))
    gii[...] = G
    tv = dot3s(xs, split(pq[:, S:])) - dot3(G, pq[:, :S])
    th[...] = tv
    h3 = chip[:, 2 * S :] - dot3(chip[:, : 2 * S], tv)
    hs[:, :S] = jnp.where(c == 0, as_rows(h3[:S]), as_rows(h3[S : 2 * S]))
    hs[:, S:] = as_rows(h3[2 * S :])


def level3_rows(minv, gii, th, ye, yx, yk, be, kb, rows, top, raw, h3, pe, qe):
    c, s, r = roles()
    o = 1 - s
    d = 1 - c
    H = S // 2
    pe[at(s, S), :] = ye[...]
    pe[at(2 * o + c, H, H), :] = yx[...]
    pe[at(2 * o + d, H, H), :] = yk[...]
    qe[at(2 * s + c, H, H), :] = be[:H]
    qe[at(2 * s + d, H, H), :] = kb[:H]
    qe[at(2 * o + c, H, H), :] = be[H:]
    qe[at(2 * o + d, H, H), :] = kb[H:]
    A = dot3(gii[...], pe[...])
    B = dot3(minv[...], qe[...])
    R_ei = split(rows[:, at(2 * (1 - r), 2 * S)])
    scale = math.sqrt(12 * S)
    R_ee = jnp.concatenate([rows[:, at(2 * r, 2 * S)], rows[:, 4 * S : 8 * S]], 1)
    own = R_ee + dot3s(R_ei, split(A))
    oth = -dot3s(R_ei, split(B))
    raw[:, at(6 * r, 6 * S)] = own
    raw[:, at(6 * (1 - r), 6 * S)] = oth
    top[...] = raw[...] * scale
    h3[...] = rows[:, 8 * S :] - dot3s(R_ei, split(th[...]))


def couple(raw, h3, mine, core, out, inc):
    c, s, r = roles()
    box_x = lax.axis_index("gx") // 4
    box_y = lax.axis_index("gy") // 2
    last_x = lax.axis_size("gx") // 4 - 1
    last_y = lax.axis_size("gy") // 2 - 1
    edge_x = (box_x == 0) | (box_x == last_x)
    edge_y = (box_y == 0) | (box_y == last_y)
    at_x = jnp.where(box_x == 0, 0, 1)
    at_y = jnp.where(box_y == 0, 0, 1)
    for n, (ss, rr) in enumerate(((s, r), (1 - s, r), (s, 1 - r), (1 - s, 1 - r))):
        lines = slice(8 * n, 8 * n + 8)
        side = jnp.where(c == 0, mine[lines, :S], core[lines, :S])
        pair = jnp.where(c == 0, core[lines, :], mine[lines, :])
        inc[:, at(6 * rr + ss, S)] = jnp.where(edge_x & (at_x == rr), 0.0, side)
        inc[:, at(6 * rr + 2 + 2 * ss, 2 * S)] = jnp.where(edge_y & (at_y == ss), 0.0, pair)
    lane = lax.broadcasted_iota(jnp.int32, (h3.shape[0], S), 1)
    total = jnp.where(lane == 0, h3[...], 0.0)
    for k in range(12):
        total = total - raw[:, k * S : (k + 1) * S] * inc[0:1, k * S : (k + 1) * S]
    lines = jnp.concatenate([total, jnp.zeros((2 * S - h3.shape[0], S), f32)], 0)
    flat = jnp.concatenate([lines[:S].T, lines[S:].T], 1)
    out[...] = jnp.sum(flat, 0, keepdims=True)[:, : h3.shape[0]]


def call(body, outs, scratch, args, us):
    whole = pl.BlockSpec(memory_space=pltpu.VMEM)
    return pl.pallas_call(
        body,
        out_shape=[jax.ShapeDtypeStruct(o, f32) for o in outs],
        in_specs=[whole] * len(args),
        out_specs=[whole] * len(outs),
        scratch_shapes=[pltpu.VMEM(x, f32) for x in scratch],
        compiler_params=pltpu.CompilerParams(vmem_limit_bytes=24 * 1024 * 1024),
        cost_estimate=pl.CostEstimate(flops=int(us * 1.15e9), bytes_accessed=0, transcendentals=0),
        name=body.__name__,
    )(*args)


def send(value, to):
    nx, ny = lax.axis_size("gx"), lax.axis_size("gy")
    pairs = []
    for i in range(nx):
        for j in range(ny):
            goal = to(i, j)
            if goal is not None and 0 <= goal[0] < nx and 0 <= goal[1] < ny:
                pairs.append((i * ny + j, goal[0] * ny + goal[1]))
    return lax.ppermute(value, ("gx", "gy"), pairs)


def after(value, *others):
    return lax.optimization_barrier((value, *others))[0]


def over_core(value):
    return send(value, lambda i, j: (i ^ 1, j))


def over_x(value):
    return send(value, lambda i, j: (i, j ^ 1))


def over_z(value):
    return send(value, lambda i, j: (i ^ 2, j))


def over_xz(value):
    return send(value, lambda i, j: (i ^ 2, j ^ 1))


def over_x_or_z(value):
    return send(value, lambda i, j: (i ^ 2, j) if i % 2 else (i, j ^ 1))


def over_edge(value):
    nx, ny = lax.axis_size("gx"), lax.axis_size("gy")

    def to(i, j):
        if i % 2 == 0:
            return ((i + 2) % nx if (i // 2) % 2 else (i - 2) % nx, j)
        return (i, (j + 1) % ny if j % 2 else (j - 1) % ny)

    return send(value, to)


def local(leaf_map, source_trace, tile_class, absorb_table):
    H = S // 2
    leaf = leaf_map[0, 0]
    oth = over_core(leaf)
    classes = tile_class[0, 0]
    chosen = (classes[:, None] == jnp.arange(absorb_table.shape[0], dtype=jnp.int32)[None, :]).astype(f32)
    levels = jnp.sum(chosen * absorb_table[None, :], axis=1)
    seg = leaf.shape[0] // classes.shape[0]
    spread = jnp.broadcast_to(levels[:, None], (classes.shape[0], seg)).reshape(-1)
    hown = (spread * source_trace[0, 0])[None]
    hoth = over_core(hown)
    (mark,) = call(bring, [(8, S)], [], [leaf], 1.0)
    minv1, pii, xi = call(
        level1_interface, [(S, S), (2 * S, 2 * S), (S + 8, 2 * S)], [], [leaf, oth, hown, hoth, mark], 2.5
    )
    xin = over_x(xi)
    m1, xe, xl = call(
        level1_map, [(6 * S, 7 * S), (S, 4 * S), (H, 5 * S)], [], [leaf, oth, hown, hoth, minv1], 2.0
    )
    xen = over_x(xe)
    xic = over_core(after(xin, xe))
    minv, gii = call(level2_inverse, [(2 * S, 2 * S)] * 2, [(2 * S, 2 * S)], [pii, xin, xic], 0.5)
    xec = over_core(after(xen, minv))
    xln = over_x(after(xl, xen, minv))
    yi, yh, yd = call(
        level2_interface,
        [(S + 8, 2 * S), (H + 8, 2 * S), (S, S)],
        [(2 * S, 2 * S)],
        [minv, gii, m1, xin, xic, xen, xec],
        1.0,
    )
    a1, a2 = over_x_or_z(yi), over_xz(yh)
    t, ye, chip, rr = call(
        level2_rest,
        [(2 * S, 9 * S), (S, 6 * S), (3 * S, 3 * S), (H + 8, 6 * S)],
        [(2 * S, 5 * S)],
        [after(minv, yd), gii, m1, xin, xic, xen, xec],
        0.01,
    )
    be, yx = call(level2_edge, [(S, 6 * S), (H, 6 * S)], [], [t, m1, ye, xln], 0.01)
    a1, a2, _, chip = lax.optimization_barrier((a1, a2, be, chip))
    k1, k2 = over_core(a1), over_core(a2)
    bn = over_z(be)
    rn = over_x(after(rr, be))
    minv3, gii3, th, hs = call(
        level3_inverse,
        [(2 * S, 2 * S), (2 * S, 2 * S), (2 * S, S), (8, 2 * S)],
        [(2 * S, 2 * S)] * 3,
        [yi, yd, a1, k1, a2, k2, chip],
        20.0,
    )
    g0 = over_edge(hs)
    rc = over_core(after(rn, minv3))
    yk = over_core(after(yx, minv3))
    (rows,) = call(level2_rows, [(3 * H, 9 * S)], [(3 * H, 7 * S)], [t, m1, rn, rc], 1.5)
    bn, g0, rows = lax.optimization_barrier((bn, g0, rows))
    kb = over_core(bn)
    gx, gz, gd = over_x(g0), over_z(g0), over_xz(g0)
    top, raw, h3 = call(
        level3_rows,
        [(3 * H, 12 * S), (3 * H, 12 * S), (3 * H, S)],
        [(2 * S, 6 * S)] * 2,
        [minv3, gii3, th, ye, yx, yk, bn, kb, rows],
        2.5,
    )
    g0, gx, gz, gd, h3 = lax.optimization_barrier((g0, gx, gz, gd, h3))
    edges = jnp.concatenate([g0, gx, gz, gd], 0)
    (out,) = call(couple, [(1, 3 * H)], [(8, 12 * S)], [raw, h3, edges, over_core(edges)], 0.7)
    return top[None, None], out[None]


def solution(mesh):
    return jax.shard_map(
        local,
        mesh=mesh,
        in_specs=(P("gx", "gy", None, None), P("gx", "gy", None), P("gx", "gy", None), P()),
        out_specs=(P("gx", "gy", None, None), P("gx", "gy", None)),
        check_vma=False,
    )
```

```python
import math

import jax
import jax.numpy as jnp
from jax import lax
from jax.experimental import pallas as pl
from jax.experimental.pallas import tpu as pltpu
from jax.sharding import PartitionSpec as P

S = 128
f32 = jnp.float32
bf16 = jnp.bfloat16
HIGHEST = lax.Precision.HIGHEST


def roles():
    gx = lax.axis_index("gx")
    gy = lax.axis_index("gy")
    return gx % 2, gy % 2, (gx // 2) % 2


def at(offset, size, unit=S):
    return pl.ds(pl.multiple_of(offset * unit, unit), size)


def split(x):
    high = x.astype(bf16)
    return high, (x - high.astype(f32)).astype(bf16)


def mm(a, b):
    return jnp.dot(a, b, preferred_element_type=f32)


def dot3s(a, b):
    return mm(a[0], b[0]) + (mm(a[0], b[1]) + mm(a[1], b[0]))


def dot3(a, b):
    return dot3s(split(a), split(b))


def dot_full(a, b):
    return jnp.dot(a, b, precision=HIGHEST, preferred_element_type=f32)


def inverse(K):
    n = K.shape[0]
    rows = lax.broadcasted_iota(jnp.int32, (n, n), 0)
    cols = lax.broadcasted_iota(jnp.int32, (n, n), 1)
    eye = (rows == cols).astype(f32)
    ks = split(K)
    X = eye + K
    power = mm(ks[0], ks[0])
    steps = 6
    for j in range(1, steps + 1):
        pb = power.astype(bf16)
        if j < steps:
            both = mm(jnp.concatenate([X.astype(bf16), pb], 0), pb)
            X = X + both[:n]
            power = both[n:]
        else:
            X = X + mm(X.astype(bf16), pb)
    xs = split(X)
    residual = eye - X + dot3s(ks, xs)
    X = X + mm(xs[0], residual.astype(bf16))
    residual = eye - X + dot_full(K, X)
    return X + dot3(X, residual)


def as_columns(row):
    return jnp.broadcast_to(row, (S, S)).T


def as_rows(block):
    return block.T[:8]


def bring(leaf, mark):
    mark[...] = leaf[:8, :S]


def level1_interface(own, oth, hown, hoth, mark, minv, pii, xi):
    c, s, r = roles()
    d = 1 - c
    e = 3 - s
    P_ii = own[at(d, S), at(d, S)]
    Q_ii = split(oth[at(c, S), at(c, S)])
    P_ie = own[at(d, S), at(e, S)]
    Q_ie = oth[at(c, S), at(e, S)]
    p_i = as_columns(hown[:, at(d, S)])
    q_i = as_columns(hoth[:, at(c, S)])
    X = inverse(dot_full(oth[at(c, S), at(c, S)], P_ii))
    minv[...] = X
    U = dot3s(Q_ii, split(jnp.concatenate([P_ie, p_i], 1)))
    T = split(dot3(X, jnp.concatenate([-U[:, :S], Q_ie, q_i - U[:, S:]], 1)))
    D = dot3s(split(own[at(e, S), at(d, S)]), T)
    Tp = jnp.concatenate([P_ie, jnp.zeros((S, S), f32)], 1) - dot3s(split(P_ii), (T[0][:, : 2 * S], T[1][:, : 2 * S]))
    DQ = dot3(oth[at(e, S), at(c, S)], Tp)
    pii[at(c, S), at(c, S)] = own[at(e, S), at(e, S)] - D[:, :S]
    pii[at(c, S), at(d, S)] = -D[:, S : 2 * S]
    pii[at(d, S), at(c, S)] = -DQ[:, :S]
    pii[at(d, S), at(d, S)] = oth[at(e, S), at(e, S)] - DQ[:, S:]
    xi[:S] = pii[at(c, S), :]
    xi[S:, :S] = as_rows(as_columns(hown[:, at(e, S)]) - D[:, 2 * S :])
    xi[S:, S:] = jnp.zeros((8, S), f32)


def level1_map(own, oth, hown, hoth, minv, m1, xe, xl):
    c, s, r = roles()
    d = 1 - c
    P_ii = own[at(d, S), at(d, S)]
    Q_ii = oth[at(c, S), at(c, S)]
    P_ie = jnp.concatenate([own[at(d, S), at(c, S)], own[at(d, S), 2 * S :]], 1)
    Q_ie = jnp.concatenate([oth[at(c, S), at(d, S)], oth[at(c, S), 2 * S :]], 1)
    p_i = as_columns(hown[:, at(d, S)])
    q_i = as_columns(hoth[:, at(c, S)])
    U = dot3(Q_ii, jnp.concatenate([P_ie, p_i], 1))
    Z = jnp.concatenate([-U[:, : 3 * S], Q_ie, q_i - U[:, 3 * S :]], 1)
    T = dot3(minv[...], Z)
    ts = split(T)
    Tp = jnp.concatenate([P_ie, jnp.zeros((S, 3 * S), f32), p_i], 1) - dot3s(split(P_ii), ts)
    P_ei = jnp.concatenate([own[at(c, S), at(d, S)], own[2 * S :, at(d, S)]], 0)
    Q_ei = jnp.concatenate([oth[at(d, S), at(c, S)], oth[2 * S :, at(c, S)]], 0)
    DP = dot3s(split(P_ei), ts)
    DQ = dot3(Q_ei, Tp)
    for k in range(3):
        mine = slice(k * S, (k + 1) * S)
        row_own = at(c, S) if k == 0 else slice((k + 1) * S, (k + 2) * S)
        row_oth = at(d, S) if k == 0 else slice((k + 1) * S, (k + 2) * S)
        to_own = at(c + 2 * k, S)
        to_oth = at(d + 2 * k, S)
        for n in range(3):
            col_own = at(c, S) if n == 0 else slice((n + 1) * S, (n + 2) * S)
            col_oth = at(d, S) if n == 0 else slice((n + 1) * S, (n + 2) * S)
            n_own = slice(n * S, (n + 1) * S)
            n_oth = slice((n + 3) * S, (n + 4) * S)
            m1[to_own, at(c + 2 * n, S)] = own[row_own, col_own] - DP[mine, n_own]
            m1[to_own, at(d + 2 * n, S)] = -DP[mine, n_oth]
            m1[to_oth, at(d + 2 * n, S)] = oth[row_oth, col_oth] - DQ[mine, n_oth]
            m1[to_oth, at(c + 2 * n, S)] = -DQ[mine, n_own]
        h_own = hown[:, at(c, S)] if k == 0 else hown[:, (k + 1) * S : (k + 2) * S]
        h_oth = hoth[:, at(d, S)] if k == 0 else hoth[:, (k + 1) * S : (k + 2) * S]
        m1[to_own, 6 * S :] = as_columns(h_own) - DP[mine, 6 * S :]
        m1[to_oth, 6 * S :] = as_columns(h_oth) - DQ[mine, 6 * S :]
    row = at(2 * (2 - s) + c, S)
    xe[:, : 2 * S] = m1[row, : 2 * S]
    xe[:, 2 * S :] = m1[row, at(2 * (1 + s), 2 * S)]
    half = at(2 * (1 - r) + c, S // 2, S // 2)
    xl[:, :S] = m1[half, at(r, S)]
    xl[:, S:] = m1[half, 2 * S : 6 * S]


def pick(x, s, low, high):
    return jnp.where(s == 0, x[:, 2 * S * low : 2 * S * (low + 1)], x[:, 2 * S * high : 2 * S * (high + 1)])


def level2_inverse(pii, xin, xic, minv, gii, qii):
    c, s, r = roles()
    qii[at(c, S), :] = xin[:S]
    qii[at(1 - c, S), :] = xic[:S]
    X = inverse(dot_full(qii[...], pii[...]))
    minv[...] = X
    gii[...] = dot3(X, qii[...])


def level2_interface(minv, gii, m1, xin, xic, xen, xec, yi, yh, yd, qe):
    c, s, r = roles()
    d = 1 - c
    H = S // 2
    inner = at(2 * (2 - s), 2 * S)
    side = at(1 - r, S)
    A = dot3(gii[...], jnp.concatenate([m1[inner, side], m1[inner, 6 * S :]], 1))
    qe[at(c, S), :S] = xen[:, side]
    qe[at(d, S), :S] = xec[:, side]
    qe[at(c, S), S:] = as_columns(xin[S : S + 1, :S])
    qe[at(d, S), S:] = as_columns(xic[S : S + 1, :S])
    B = dot3(minv[...], qe[...])
    D = dot3(m1[side, inner], jnp.concatenate([A[:, :S], B[:, :S], B[:, S:] - A[:, S:]], 1))
    data = m1[side, 6 * S :] - D[:, 2 * S :]
    yd[...] = data
    yi[:S, at(s, S)] = m1[side, side] + D[:, :S]
    yi[:S, at(1 - s, S)] = -D[:, S : 2 * S]
    yi[S:, :S] = as_rows(data)
    yi[S:, S:] = jnp.zeros((8, S), f32)
    yh[:H] = yi[at(c, H, H), :]
    yh[H:] = yi[S:]


def level2_rest(minv, gii, m1, xin, xic, xen, xec, t, ye, chip, rr, qe):
    c, s, r = roles()
    o = 1 - s
    H = S // 2
    inner = at(2 * (2 - s), 2 * S)
    outer = at(2 * (1 + s), 2 * S)
    P_e = jnp.concatenate([m1[inner, : 2 * S], m1[inner, outer], m1[inner, 6 * S :]], 1)
    A = dot3(gii[...], P_e)
    qe[at(c, S), : 4 * S] = xen[...]
    qe[at(1 - c, S), : 4 * S] = xec[...]
    qe[at(c, S), 4 * S :] = as_columns(xin[S : S + 1, :S])
    qe[at(1 - c, S), 4 * S :] = as_columns(xic[S : S + 1, :S])
    B = dot3(minv[...], qe[...])
    t[:, at(s, S)] = -A[:, :S]
    t[:, at(2 + s, S)] = -A[:, S : 2 * S]
    t[:, at(4 + 2 * s, 2 * S)] = -A[:, 2 * S : 4 * S]
    t[:, at(o, S)] = B[:, :S]
    t[:, at(2 + o, S)] = B[:, S : 2 * S]
    t[:, at(4 + 2 * o, 2 * S)] = B[:, 2 * S : 4 * S]
    t[:, 8 * S :] = B[:, 4 * S :] - A[:, 4 * S :]
    row = at(1 - r, S)
    ye[...] = -dot3(m1[row, inner], jnp.concatenate([t[:, at(2 * r, 2 * S)], t[:, 4 * S : 8 * S]], 1))
    ye[:, at(s, S)] += m1[row, at(r, S)]
    ye[:, at(2 + 2 * s, 2 * S)] += m1[row, outer]
    P_ei = jnp.concatenate([m1[at(r, S), inner], m1[outer, inner]], 0)
    T_i = jnp.concatenate([t[:, at(2 * (1 - r), 2 * S)], t[:, 8 * S :]], 1)
    chip[...] = -dot3(P_ei, T_i)
    chip[:S, at(s, S)] += m1[at(r, S), at(1 - r, S)]
    chip[S:, at(s, S)] += m1[outer, at(1 - r, S)]
    chip[:S, 2 * S :] += m1[at(r, S), 6 * S :]
    chip[S:, 2 * S :] += m1[outer, 6 * S :]
    first = jnp.where(c == 0, jnp.where(s == 0, 4, 2 * r), jnp.where(s == 0, 5, 8))
    lines = at(first, H, H)
    rr[:H] = m1[lines, : 6 * S]
    rr[H:, :S] = as_rows(jnp.concatenate([m1[lines, 6 * S :]] * 2, 0))
    rr[H:, S:] = jnp.zeros((8, 5 * S), f32)


def level2_edge(t, m1, ye, xln, be, yx):
    c, s, r = roles()
    o = 1 - s
    H = S // 2
    inner = at(2 * (2 - s), 2 * S)
    link = pick(xln[:, S:], s, 0, 1)
    V = dot3(link, m1[inner, : 6 * S])
    D = dot3(pick(V, s, 2, 1), jnp.concatenate([t[:, at(2 * r, 2 * S)], t[:, 4 * S : 8 * S]], 1))
    yx[...] = D
    yx[:, at(s, S)] -= jnp.where(r == 0, V[:, :S], V[:, S : 2 * S])
    yx[:, at(2 + 2 * s, 2 * S)] -= pick(V, s, 1, 2)
    yx[:, at(o, S)] += xln[:, :S]
    yx[:, at(2 + 2 * o, 2 * S)] += pick(xln[:, S:], s, 1, 0)
    be[:H] = ye[at(c, H, H), :]
    be[H:] = yx[...]


def level2_rows(t, m1, rn, rc, rows, work):
    c, s, r = roles()
    o = 1 - s
    H = S // 2
    inner = at(2 * (2 - s), 2 * S)
    outer = at(2 * (1 + s), 2 * S)
    m = 2 * c + s

    @pl.when(m == 0)
    def _():
        work[: 2 * H] = m1[at(2 * r, 2 * H, H), :]

    @pl.when(m == 1)
    def _():
        work[:H] = m1[at(2 * r + 1, H, H), :]
        work[H : 2 * H, : 6 * S] = rn[:H]
        work[H : 2 * H, 6 * S :] = as_columns(rn[H : H + 1, :S])[:H]
        work[2 * H :, : 6 * S] = rc[:H]
        work[2 * H :, 6 * S :] = as_columns(rc[H : H + 1, :S])[:H]

    @pl.when(m == 2)
    def _():
        work[: 2 * H] = m1[6 * H : 8 * H, :]

    @pl.when((m == 0) | (m == 2))
    def _():
        work[2 * H :, : 6 * S] = rn[:H]
        work[2 * H :, 6 * S :] = as_columns(rn[H : H + 1, :S])[:H]

    @pl.when(m == 3)
    def _():
        work[...] = m1[9 * H : 12 * H, :]

    start = jnp.where(m == 1, H, jnp.where(m == 3, 3 * H, 2 * H))
    index = lax.broadcasted_iota(jnp.int32, (3 * H, 1), 0)
    got = index >= start
    V = dot3(work[:, outer], m1[inner, :])
    rows[:, : 7 * S] = V
    V_ii = rows[:, inner]
    V_pair = rows[:, outer]
    C = jnp.where(got, V_ii, -work[:, inner])
    D = dot3(C, t[...])
    own_side = jnp.where(got, -V[:, : 2 * S], work[:, : 2 * S])
    own_pair = jnp.where(got, -V_pair, work[:, outer])
    oth_side = jnp.where(got, work[:, : 2 * S], 0.0)
    oth_pair = jnp.where(got, work[:, inner], 0.0)
    data = work[:, 6 * S :] - jnp.where(got, V[:, 6 * S :], 0.0)
    rows[...] = D
    rows[:, at(s, S)] += own_side[:, :S]
    rows[:, at(2 + s, S)] += own_side[:, S:]
    rows[:, at(4 + 2 * s, 2 * S)] += own_pair
    rows[:, at(o, S)] += oth_side[:, :S]
    rows[:, at(2 + o, S)] += oth_side[:, S:]
    rows[:, at(4 + 2 * o, 2 * S)] += oth_pair
    rows[:, 8 * S :] += data


def level3_inverse(yi, yd, a1, k1, a2, k2, chip, minv, gii, th, hs, pii, qii, pq):
    c, s, r = roles()
    o = 1 - s
    d = 1 - c
    H = S // 2
    x = jnp.where(c == 0, a1[...], k1[...])
    z = jnp.where(c == 0, k1[...], a1[...])
    pii[at(s, S), :] = yi[:S]
    pii[at(o, S), :] = x[:S]
    qii[at(s, S), :] = z[:S]
    qii[at(2 * o + c, H, H), :] = a2[:H]
    qii[at(2 * o + d, H, H), :] = k2[:H]
    pq[at(s, S), :S] = yd[...]
    pq[at(o, S), :S] = as_columns(x[S : S + 1, :S])
    pq[at(s, S), S:] = as_columns(z[S : S + 1, :S])
    pq[at(o, S), S:] = as_columns(a2[H : H + 1, :S])
    X = inverse(dot_full(qii[...], pii[...]))
    xs = split(X)
    minv[...] = X
    G = dot3s(xs, split(qii[...]))
    gii[...] = G
    tv = dot3s(xs, split(pq[:, S:])) - dot3(G, pq[:, :S])
    th[...] = tv
    h3 = chip[:, 2 * S :] - dot3(chip[:, : 2 * S], tv)
    hs[:, :S] = jnp.where(c == 0, as_rows(h3[:S]), as_rows(h3[S : 2 * S]))
    hs[:, S:] = as_rows(h3[2 * S :])


def level3_rows(minv, gii, th, ye, yx, yk, be, kb, rows, top, raw, h3, pe, qe):
    c, s, r = roles()
    o = 1 - s
    d = 1 - c
    H = S // 2
    pe[at(s, S), :] = ye[...]
    pe[at(2 * o + c, H, H), :] = yx[...]
    pe[at(2 * o + d, H, H), :] = yk[...]
    qe[at(2 * s + c, H, H), :] = be[:H]
    qe[at(2 * s + d, H, H), :] = kb[:H]
    qe[at(2 * o + c, H, H), :] = be[H:]
    qe[at(2 * o + d, H, H), :] = kb[H:]
    A = dot3(gii[...], pe[...])
    B = dot3(minv[...], qe[...])
    R_ei = split(rows[:, at(2 * (1 - r), 2 * S)])
    scale = math.sqrt(12 * S)
    R_ee = jnp.concatenate([rows[:, at(2 * r, 2 * S)], rows[:, 4 * S : 8 * S]], 1)
    own = R_ee + dot3s(R_ei, split(A))
    oth = -dot3s(R_ei, split(B))
    raw[:, at(6 * r, 6 * S)] = own
    raw[:, at(6 * (1 - r), 6 * S)] = oth
    top[...] = raw[...] * scale
    h3[...] = rows[:, 8 * S :] - dot3s(R_ei, split(th[...]))


def couple(raw, h3, mine, core, out, inc):
    c, s, r = roles()
    box_x = lax.axis_index("gx") // 4
    box_y = lax.axis_index("gy") // 2
    last_x = lax.axis_size("gx") // 4 - 1
    last_y = lax.axis_size("gy") // 2 - 1
    edge_x = (box_x == 0) | (box_x == last_x)
    edge_y = (box_y == 0) | (box_y == last_y)
    at_x = jnp.where(box_x == 0, 0, 1)
    at_y = jnp.where(box_y == 0, 0, 1)
    for n, (ss, rr) in enumerate(((s, r), (1 - s, r), (s, 1 - r), (1 - s, 1 - r))):
        lines = slice(8 * n, 8 * n + 8)
        side = jnp.where(c == 0, mine[lines, :S], core[lines, :S])
        pair = jnp.where(c == 0, core[lines, :], mine[lines, :])
        inc[:, at(6 * rr + ss, S)] = jnp.where(edge_x & (at_x == rr), 0.0, side)
        inc[:, at(6 * rr + 2 + 2 * ss, 2 * S)] = jnp.where(edge_y & (at_y == ss), 0.0, pair)
    lane = lax.broadcasted_iota(jnp.int32, (h3.shape[0], S), 1)
    total = jnp.where(lane == 0, h3[...], 0.0)
    for k in range(12):
        total = total - raw[:, k * S : (k + 1) * S] * inc[0:1, k * S : (k + 1) * S]
    lines = jnp.concatenate([total, jnp.zeros((2 * S - h3.shape[0], S), f32)], 0)
    flat = jnp.concatenate([lines[:S].T, lines[S:].T], 1)
    out[...] = jnp.sum(flat, 0, keepdims=True)[:, : h3.shape[0]]


def call(body, outs, scratch, args, us):
    whole = pl.BlockSpec(memory_space=pltpu.VMEM)
    return pl.pallas_call(
        body,
        out_shape=[jax.ShapeDtypeStruct(o, f32) for o in outs],
        in_specs=[whole] * len(args),
        out_specs=[whole] * len(outs),
        scratch_shapes=[pltpu.VMEM(x, f32) for x in scratch],
        compiler_params=pltpu.CompilerParams(vmem_limit_bytes=24 * 1024 * 1024),
        cost_estimate=pl.CostEstimate(flops=int(us * 1.15e9), bytes_accessed=0, transcendentals=0),
        name=body.__name__,
    )(*args)


def send(value, to):
    nx, ny = lax.axis_size("gx"), lax.axis_size("gy")
    pairs = []
    for i in range(nx):
        for j in range(ny):
            goal = to(i, j)
            if goal is not None and 0 <= goal[0] < nx and 0 <= goal[1] < ny:
                pairs.append((i * ny + j, goal[0] * ny + goal[1]))
    return lax.ppermute(value, ("gx", "gy"), pairs)


def after(value, *others):
    return lax.optimization_barrier((value, *others))[0]


def over_core(value):
    return send(value, lambda i, j: (i ^ 1, j))


def over_x(value):
    return send(value, lambda i, j: (i, j ^ 1))


def over_z(value):
    return send(value, lambda i, j: (i ^ 2, j))


def over_xz(value):
    return send(value, lambda i, j: (i ^ 2, j ^ 1))


def over_x_or_z(value):
    return send(value, lambda i, j: (i ^ 2, j) if i % 2 else (i, j ^ 1))


def over_edge(value):
    nx, ny = lax.axis_size("gx"), lax.axis_size("gy")

    def to(i, j):
        if i % 2 == 0:
            return ((i + 2) % nx if (i // 2) % 2 else (i - 2) % nx, j)
        return (i, (j + 1) % ny if j % 2 else (j - 1) % ny)

    return send(value, to)


def local(leaf_map, source_trace, tile_class, absorb_table):
    H = S // 2
    leaf = leaf_map[0, 0]
    oth = over_core(leaf)
    classes = tile_class[0, 0]
    chosen = (classes[:, None] == jnp.arange(absorb_table.shape[0], dtype=jnp.int32)[None, :]).astype(f32)
    levels = jnp.sum(chosen * absorb_table[None, :], axis=1)
    seg = leaf.shape[0] // classes.shape[0]
    spread = jnp.broadcast_to(levels[:, None], (classes.shape[0], seg)).reshape(-1)
    hown = (spread * source_trace[0, 0])[None]
    hoth = over_core(hown)
    (mark,) = call(bring, [(8, S)], [], [leaf], 1.0)
    minv1, pii, xi = call(
        level1_interface, [(S, S), (2 * S, 2 * S), (S + 8, 2 * S)], [], [leaf, oth, hown, hoth, mark], 2.5
    )
    xin = over_x(xi)
    m1, xe, xl = call(
        level1_map, [(6 * S, 7 * S), (S, 4 * S), (H, 5 * S)], [], [leaf, oth, hown, hoth, minv1], 2.0
    )
    xen = over_x(xe)
    xic = over_core(after(xin, xe))
    minv, gii = call(level2_inverse, [(2 * S, 2 * S)] * 2, [(2 * S, 2 * S)], [pii, xin, xic], 0.5)
    xec = over_core(after(xen, minv))
    xln = over_x(after(xl, xen, minv))
    yi, yh, yd = call(
        level2_interface,
        [(S + 8, 2 * S), (H + 8, 2 * S), (S, S)],
        [(2 * S, 2 * S)],
        [minv, gii, m1, xin, xic, xen, xec],
        1.0,
    )
    a1, a2 = over_x_or_z(yi), over_xz(yh)
    t, ye, chip, rr = call(
        level2_rest,
        [(2 * S, 9 * S), (S, 6 * S), (3 * S, 3 * S), (H + 8, 6 * S)],
        [(2 * S, 5 * S)],
        [after(minv, yd), gii, m1, xin, xic, xen, xec],
        0.01,
    )
    be, yx = call(level2_edge, [(S, 6 * S), (H, 6 * S)], [], [t, m1, ye, xln], 0.01)
    a1, a2, _, chip = lax.optimization_barrier((a1, a2, be, chip))
    k1, k2 = over_core(a1), over_core(a2)
    bn = over_z(be)
    rn = over_x(after(rr, be))
    minv3, gii3, th, hs = call(
        level3_inverse,
        [(2 * S, 2 * S), (2 * S, 2 * S), (2 * S, S), (8, 2 * S)],
        [(2 * S, 2 * S)] * 3,
        [yi, yd, a1, k1, a2, k2, chip],
        0.3,
    )
    g0 = over_edge(hs)
    rc = over_core(after(rn, minv3))
    yk = over_core(after(yx, minv3))
    (rows,) = call(level2_rows, [(3 * H, 9 * S)], [(3 * H, 7 * S)], [t, m1, rn, rc], 1.5)
    bn, g0, rows = lax.optimization_barrier((bn, g0, rows))
    kb = over_core(bn)
    gx, gz, gd = over_x(g0), over_z(g0), over_xz(g0)
    top, raw, h3 = call(
        level3_rows,
        [(3 * H, 12 * S), (3 * H, 12 * S), (3 * H, S)],
        [(2 * S, 6 * S)] * 2,
        [minv3, gii3, th, ye, yx, yk, bn, kb, rows],
        2.5,
    )
    g0, gx, gz, gd, h3 = lax.optimization_barrier((g0, gx, gz, gd, h3))
    edges = jnp.concatenate([g0, gx, gz, gd], 0)
    (out,) = call(couple, [(1, 3 * H)], [(8, 12 * S)], [raw, h3, edges, over_core(edges)], 0.7)
    return top[None, None], out[None]


def solution(mesh):
    return jax.shard_map(
        local,
        mesh=mesh,
        in_specs=(P("gx", "gy", None, None), P("gx", "gy", None), P("gx", "gy", None), P()),
        out_specs=(P("gx", "gy", None, None), P("gx", "gy", None)),
        check_vma=False,
    )
```

```python
import math

import jax
import jax.numpy as jnp
from jax import lax
from jax.experimental import pallas as pl
from jax.experimental.pallas import tpu as pltpu
from jax.sharding import PartitionSpec as P

S = 128
f32 = jnp.float32
bf16 = jnp.bfloat16
HIGHEST = lax.Precision.HIGHEST


def roles():
    gx = lax.axis_index("gx")
    gy = lax.axis_index("gy")
    return gx % 2, gy % 2, (gx // 2) % 2


def at(offset, size, unit=S):
    return pl.ds(pl.multiple_of(offset * unit, unit), size)


def split(x):
    high = x.astype(bf16)
    return high, (x - high.astype(f32)).astype(bf16)


def mm(a, b):
    return jnp.dot(a, b, preferred_element_type=f32)


def dot3s(a, b):
    return mm(a[0], b[0]) + (mm(a[0], b[1]) + mm(a[1], b[0]))


def dot3(a, b):
    return dot3s(split(a), split(b))


def dot_full(a, b):
    return jnp.dot(a, b, precision=HIGHEST, preferred_element_type=f32)


def inverse(K):
    n = K.shape[0]
    rows = lax.broadcasted_iota(jnp.int32, (n, n), 0)
    cols = lax.broadcasted_iota(jnp.int32, (n, n), 1)
    eye = (rows == cols).astype(f32)
    ks = split(K)
    X = eye + K
    power = mm(ks[0], ks[0])
    steps = 6
    for j in range(1, steps + 1):
        pb = power.astype(bf16)
        if j < steps:
            both = mm(jnp.concatenate([X.astype(bf16), pb], 0), pb)
            X = X + both[:n]
            power = both[n:]
        else:
            X = X + mm(X.astype(bf16), pb)
    xs = split(X)
    residual = eye - X + dot3s(ks, xs)
    X = X + mm(xs[0], residual.astype(bf16))
    residual = eye - X + dot_full(K, X)
    return X + dot3(X, residual)


def as_columns(row):
    return jnp.broadcast_to(row, (S, S)).T


def as_rows(block):
    return block.T[:8]


def bring(leaf, mark):
    mark[...] = leaf[:8, :S]


def level1_interface(own, oth, hown, hoth, mark, minv, pii, xi):
    c, s, r = roles()
    d = 1 - c
    e = 3 - s
    P_ii = own[at(d, S), at(d, S)]
    Q_ii = split(oth[at(c, S), at(c, S)])
    P_ie = own[at(d, S), at(e, S)]
    Q_ie = oth[at(c, S), at(e, S)]
    p_i = as_columns(hown[:, at(d, S)])
    q_i = as_columns(hoth[:, at(c, S)])
    X = inverse(dot_full(oth[at(c, S), at(c, S)], P_ii))
    minv[...] = X
    U = dot3s(Q_ii, split(jnp.concatenate([P_ie, p_i], 1)))
    T = split(dot3(X, jnp.concatenate([-U[:, :S], Q_ie, q_i - U[:, S:]], 1)))
    D = dot3s(split(own[at(e, S), at(d, S)]), T)
    Tp = jnp.concatenate([P_ie, jnp.zeros((S, S), f32)], 1) - dot3s(split(P_ii), (T[0][:, : 2 * S], T[1][:, : 2 * S]))
    DQ = dot3(oth[at(e, S), at(c, S)], Tp)
    pii[at(c, S), at(c, S)] = own[at(e, S), at(e, S)] - D[:, :S]
    pii[at(c, S), at(d, S)] = -D[:, S : 2 * S]
    pii[at(d, S), at(c, S)] = -DQ[:, :S]
    pii[at(d, S), at(d, S)] = oth[at(e, S), at(e, S)] - DQ[:, S:]
    xi[:S] = pii[at(c, S), :]
    xi[S:, :S] = as_rows(as_columns(hown[:, at(e, S)]) - D[:, 2 * S :])
    xi[S:, S:] = jnp.zeros((8, S), f32)


def level1_map(own, oth, hown, hoth, minv, m1, xe, xl):
    c, s, r = roles()
    d = 1 - c
    P_ii = own[at(d, S), at(d, S)]
    Q_ii = oth[at(c, S), at(c, S)]
    P_ie = jnp.concatenate([own[at(d, S), at(c, S)], own[at(d, S), 2 * S :]], 1)
    Q_ie = jnp.concatenate([oth[at(c, S), at(d, S)], oth[at(c, S), 2 * S :]], 1)
    p_i = as_columns(hown[:, at(d, S)])
    q_i = as_columns(hoth[:, at(c, S)])
    U = dot3(Q_ii, jnp.concatenate([P_ie, p_i], 1))
    Z = jnp.concatenate([-U[:, : 3 * S], Q_ie, q_i - U[:, 3 * S :]], 1)
    T = dot3(minv[...], Z)
    ts = split(T)
    Tp = jnp.concatenate([P_ie, jnp.zeros((S, 3 * S), f32), p_i], 1) - dot3s(split(P_ii), ts)
    P_ei = jnp.concatenate([own[at(c, S), at(d, S)], own[2 * S :, at(d, S)]], 0)
    Q_ei = jnp.concatenate([oth[at(d, S), at(c, S)], oth[2 * S :, at(c, S)]], 0)
    DP = dot3s(split(P_ei), ts)
    DQ = dot3(Q_ei, Tp)
    for k in range(3):
        mine = slice(k * S, (k + 1) * S)
        row_own = at(c, S) if k == 0 else slice((k + 1) * S, (k + 2) * S)
        row_oth = at(d, S) if k == 0 else slice((k + 1) * S, (k + 2) * S)
        to_own = at(c + 2 * k, S)
        to_oth = at(d + 2 * k, S)
        for n in range(3):
            col_own = at(c, S) if n == 0 else slice((n + 1) * S, (n + 2) * S)
            col_oth = at(d, S) if n == 0 else slice((n + 1) * S, (n + 2) * S)
            n_own = slice(n * S, (n + 1) * S)
            n_oth = slice((n + 3) * S, (n + 4) * S)
            m1[to_own, at(c + 2 * n, S)] = own[row_own, col_own] - DP[mine, n_own]
            m1[to_own, at(d + 2 * n, S)] = -DP[mine, n_oth]
            m1[to_oth, at(d + 2 * n, S)] = oth[row_oth, col_oth] - DQ[mine, n_oth]
            m1[to_oth, at(c + 2 * n, S)] = -DQ[mine, n_own]
        h_own = hown[:, at(c, S)] if k == 0 else hown[:, (k + 1) * S : (k + 2) * S]
        h_oth = hoth[:, at(d, S)] if k == 0 else hoth[:, (k + 1) * S : (k + 2) * S]
        m1[to_own, 6 * S :] = as_columns(h_own) - DP[mine, 6 * S :]
        m1[to_oth, 6 * S :] = as_columns(h_oth) - DQ[mine, 6 * S :]
    row = at(2 * (2 - s) + c, S)
    xe[:, : 2 * S] = m1[row, : 2 * S]
    xe[:, 2 * S :] = m1[row, at(2 * (1 + s), 2 * S)]
    half = at(2 * (1 - r) + c, S // 2, S // 2)
    xl[:, :S] = m1[half, at(r, S)]
    xl[:, S:] = m1[half, 2 * S : 6 * S]


def pick(x, s, low, high):
    return jnp.where(s == 0, x[:, 2 * S * low : 2 * S * (low + 1)], x[:, 2 * S * high : 2 * S * (high + 1)])


def level2_inverse(pii, xin, xic, minv, gii, qii):
    c, s, r = roles()
    qii[at(c, S), :] = xin[:S]
    qii[at(1 - c, S), :] = xic[:S]
    X = inverse(dot_full(qii[...], pii[...]))
    minv[...] = X
    gii[...] = dot3(X, qii[...])


def level2_interface(minv, gii, m1, xin, xic, xen, xec, yi, yh, yd, qe):
    c, s, r = roles()
    d = 1 - c
    H = S // 2
    inner = at(2 * (2 - s), 2 * S)
    side = at(1 - r, S)
    A = dot3(gii[...], jnp.concatenate([m1[inner, side], m1[inner, 6 * S :]], 1))
    qe[at(c, S), :S] = xen[:, side]
    qe[at(d, S), :S] = xec[:, side]
    qe[at(c, S), S:] = as_columns(xin[S : S + 1, :S])
    qe[at(d, S), S:] = as_columns(xic[S : S + 1, :S])
    B = dot3(minv[...], qe[...])
    D = dot3(m1[side, inner], jnp.concatenate([A[:, :S], B[:, :S], B[:, S:] - A[:, S:]], 1))
    data = m1[side, 6 * S :] - D[:, 2 * S :]
    yd[...] = data
    yi[:S, at(s, S)] = m1[side, side] + D[:, :S]
    yi[:S, at(1 - s, S)] = -D[:, S : 2 * S]
    yi[S:, :S] = as_rows(data)
    yi[S:, S:] = jnp.zeros((8, S), f32)
    yh[:H] = yi[at(c, H, H), :]
    yh[H:] = yi[S:]


def level2_rest(minv, gii, m1, xin, xic, xen, xec, t, ye, chip, rr, qe):
    c, s, r = roles()
    o = 1 - s
    H = S // 2
    inner = at(2 * (2 - s), 2 * S)
    outer = at(2 * (1 + s), 2 * S)
    P_e = jnp.concatenate([m1[inner, : 2 * S], m1[inner, outer], m1[inner, 6 * S :]], 1)
    A = dot3(gii[...], P_e)
    qe[at(c, S), : 4 * S] = xen[...]
    qe[at(1 - c, S), : 4 * S] = xec[...]
    qe[at(c, S), 4 * S :] = as_columns(xin[S : S + 1, :S])
    qe[at(1 - c, S), 4 * S :] = as_columns(xic[S : S + 1, :S])
    B = dot3(minv[...], qe[...])
    t[:, at(s, S)] = -A[:, :S]
    t[:, at(2 + s, S)] = -A[:, S : 2 * S]
    t[:, at(4 + 2 * s, 2 * S)] = -A[:, 2 * S : 4 * S]
    t[:, at(o, S)] = B[:, :S]
    t[:, at(2 + o, S)] = B[:, S : 2 * S]
    t[:, at(4 + 2 * o, 2 * S)] = B[:, 2 * S : 4 * S]
    t[:, 8 * S :] = B[:, 4 * S :] - A[:, 4 * S :]
    row = at(1 - r, S)
    ye[...] = -dot3(m1[row, inner], jnp.concatenate([t[:, at(2 * r, 2 * S)], t[:, 4 * S : 8 * S]], 1))
    ye[:, at(s, S)] += m1[row, at(r, S)]
    ye[:, at(2 + 2 * s, 2 * S)] += m1[row, outer]
    P_ei = jnp.concatenate([m1[at(r, S), inner], m1[outer, inner]], 0)
    T_i = jnp.concatenate([t[:, at(2 * (1 - r), 2 * S)], t[:, 8 * S :]], 1)
    chip[...] = -dot3(P_ei, T_i)
    chip[:S, at(s, S)] += m1[at(r, S), at(1 - r, S)]
    chip[S:, at(s, S)] += m1[outer, at(1 - r, S)]
    chip[:S, 2 * S :] += m1[at(r, S), 6 * S :]
    chip[S:, 2 * S :] += m1[outer, 6 * S :]
    first = jnp.where(c == 0, jnp.where(s == 0, 4, 2 * r), jnp.where(s == 0, 5, 8))
    lines = at(first, H, H)
    rr[:H] = m1[lines, : 6 * S]
    rr[H:, :S] = as_rows(jnp.concatenate([m1[lines, 6 * S :]] * 2, 0))
    rr[H:, S:] = jnp.zeros((8, 5 * S), f32)


def level2_edge(t, m1, ye, xln, be, yx):
    c, s, r = roles()
    o = 1 - s
    H = S // 2
    inner = at(2 * (2 - s), 2 * S)
    link = pick(xln[:, S:], s, 0, 1)
    V = dot3(link, m1[inner, : 6 * S])
    D = dot3(pick(V, s, 2, 1), jnp.concatenate([t[:, at(2 * r, 2 * S)], t[:, 4 * S : 8 * S]], 1))
    yx[...] = D
    yx[:, at(s, S)] -= jnp.where(r == 0, V[:, :S], V[:, S : 2 * S])
    yx[:, at(2 + 2 * s, 2 * S)] -= pick(V, s, 1, 2)
    yx[:, at(o, S)] += xln[:, :S]
    yx[:, at(2 + 2 * o, 2 * S)] += pick(xln[:, S:], s, 1, 0)
    be[:H] = ye[at(c, H, H), :]
    be[H:] = yx[...]


def level2_rows(t, m1, rn, rc, rows, work):
    c, s, r = roles()
    o = 1 - s
    H = S // 2
    inner = at(2 * (2 - s), 2 * S)
    outer = at(2 * (1 + s), 2 * S)
    m = 2 * c + s

    @pl.when(m == 0)
    def _():
        work[: 2 * H] = m1[at(2 * r, 2 * H, H), :]

    @pl.when(m == 1)
    def _():
        work[:H] = m1[at(2 * r + 1, H, H), :]
        work[H : 2 * H, : 6 * S] = rn[:H]
        work[H : 2 * H, 6 * S :] = as_columns(rn[H : H + 1, :S])[:H]
        work[2 * H :, : 6 * S] = rc[:H]
        work[2 * H :, 6 * S :] = as_columns(rc[H : H + 1, :S])[:H]

    @pl.when(m == 2)
    def _():
        work[: 2 * H] = m1[6 * H : 8 * H, :]

    @pl.when((m == 0) | (m == 2))
    def _():
        work[2 * H :, : 6 * S] = rn[:H]
        work[2 * H :, 6 * S :] = as_columns(rn[H : H + 1, :S])[:H]

    @pl.when(m == 3)
    def _():
        work[...] = m1[9 * H : 12 * H, :]

    start = jnp.where(m == 1, H, jnp.where(m == 3, 3 * H, 2 * H))
    index = lax.broadcasted_iota(jnp.int32, (3 * H, 1), 0)
    got = index >= start
    V = dot3(work[:, outer], m1[inner, :])
    rows[:, : 7 * S] = V
    V_ii = rows[:, inner]
    V_pair = rows[:, outer]
    C = jnp.where(got, V_ii, -work[:, inner])
    D = dot3(C, t[...])
    own_side = jnp.where(got, -V[:, : 2 * S], work[:, : 2 * S])
    own_pair = jnp.where(got, -V_pair, work[:, outer])
    oth_side = jnp.where(got, work[:, : 2 * S], 0.0)
    oth_pair = jnp.where(got, work[:, inner], 0.0)
    data = work[:, 6 * S :] - jnp.where(got, V[:, 6 * S :], 0.0)
    rows[...] = D
    rows[:, at(s, S)] += own_side[:, :S]
    rows[:, at(2 + s, S)] += own_side[:, S:]
    rows[:, at(4 + 2 * s, 2 * S)] += own_pair
    rows[:, at(o, S)] += oth_side[:, :S]
    rows[:, at(2 + o, S)] += oth_side[:, S:]
    rows[:, at(4 + 2 * o, 2 * S)] += oth_pair
    rows[:, 8 * S :] += data


def level3_inverse(yi, yd, a1, k1, a2, k2, chip, minv, gii, th, hs, pii, qii, pq):
    c, s, r = roles()
    o = 1 - s
    d = 1 - c
    H = S // 2
    x = jnp.where(c == 0, a1[...], k1[...])
    z = jnp.where(c == 0, k1[...], a1[...])
    pii[at(s, S), :] = yi[:S]
    pii[at(o, S), :] = x[:S]
    qii[at(s, S), :] = z[:S]
    qii[at(2 * o + c, H, H), :] = a2[:H]
    qii[at(2 * o + d, H, H), :] = k2[:H]
    pq[at(s, S), :S] = yd[...]
    pq[at(o, S), :S] = as_columns(x[S : S + 1, :S])
    pq[at(s, S), S:] = as_columns(z[S : S + 1, :S])
    pq[at(o, S), S:] = as_columns(a2[H : H + 1, :S])
    X = inverse(dot_full(qii[...], pii[...]))
    xs = split(X)
    minv[...] = X
    G = dot3s(xs, split(qii[...]))
    gii[...] = G
    tv = dot3s(xs, split(pq[:, S:])) - dot3(G, pq[:, :S])
    th[...] = tv
    h3 = chip[:, 2 * S :] - dot3(chip[:, : 2 * S], tv)
    hs[:, :S] = jnp.where(c == 0, as_rows(h3[:S]), as_rows(h3[S : 2 * S]))
    hs[:, S:] = as_rows(h3[2 * S :])


def level3_rows(minv, gii, th, ye, yx, yk, be, kb, rows, top, raw, h3, pe, qe):
    c, s, r = roles()
    o = 1 - s
    d = 1 - c
    H = S // 2
    pe[at(s, S), :] = ye[...]
    pe[at(2 * o + c, H, H), :] = yx[...]
    pe[at(2 * o + d, H, H), :] = yk[...]
    qe[at(2 * s + c, H, H), :] = be[:H]
    qe[at(2 * s + d, H, H), :] = kb[:H]
    qe[at(2 * o + c, H, H), :] = be[H:]
    qe[at(2 * o + d, H, H), :] = kb[H:]
    A = dot3(gii[...], pe[...])
    B = dot3(minv[...], qe[...])
    R_ei = split(rows[:, at(2 * (1 - r), 2 * S)])
    scale = math.sqrt(12 * S)
    R_ee = jnp.concatenate([rows[:, at(2 * r, 2 * S)], rows[:, 4 * S : 8 * S]], 1)
    own = R_ee + dot3s(R_ei, split(A))
    oth = -dot3s(R_ei, split(B))
    raw[:, at(6 * r, 6 * S)] = own
    raw[:, at(6 * (1 - r), 6 * S)] = oth
    top[...] = raw[...] * scale
    h3[...] = rows[:, 8 * S :] - dot3s(R_ei, split(th[...]))


def couple(raw, h3, mine, core, out, inc):
    c, s, r = roles()
    box_x = lax.axis_index("gx") // 4
    box_y = lax.axis_index("gy") // 2
    last_x = lax.axis_size("gx") // 4 - 1
    last_y = lax.axis_size("gy") // 2 - 1
    edge_x = (box_x == 0) | (box_x == last_x)
    edge_y = (box_y == 0) | (box_y == last_y)
    at_x = jnp.where(box_x == 0, 0, 1)
    at_y = jnp.where(box_y == 0, 0, 1)
    for n, (ss, rr) in enumerate(((s, r), (1 - s, r), (s, 1 - r), (1 - s, 1 - r))):
        lines = slice(8 * n, 8 * n + 8)
        side = jnp.where(c == 0, mine[lines, :S], core[lines, :S])
        pair = jnp.where(c == 0, core[lines, :], mine[lines, :])
        inc[:, at(6 * rr + ss, S)] = jnp.where(edge_x & (at_x == rr), 0.0, side)
        inc[:, at(6 * rr + 2 + 2 * ss, 2 * S)] = jnp.where(edge_y & (at_y == ss), 0.0, pair)
    lane = lax.broadcasted_iota(jnp.int32, (h3.shape[0], S), 1)
    total = jnp.where(lane == 0, h3[...], 0.0)
    for k in range(12):
        total = total - raw[:, k * S : (k + 1) * S] * inc[0:1, k * S : (k + 1) * S]
    lines = jnp.concatenate([total, jnp.zeros((2 * S - h3.shape[0], S), f32)], 0)
    flat = jnp.concatenate([lines[:S].T, lines[S:].T], 1)
    out[...] = jnp.sum(flat, 0, keepdims=True)[:, : h3.shape[0]]


def call(body, outs, scratch, args, us):
    whole = pl.BlockSpec(memory_space=pltpu.VMEM)
    return pl.pallas_call(
        body,
        out_shape=[jax.ShapeDtypeStruct(o, f32) for o in outs],
        in_specs=[whole] * len(args),
        out_specs=[whole] * len(outs),
        scratch_shapes=[pltpu.VMEM(x, f32) for x in scratch],
        compiler_params=pltpu.CompilerParams(vmem_limit_bytes=24 * 1024 * 1024),
        cost_estimate=pl.CostEstimate(flops=int(us * 1.15e9), bytes_accessed=0, transcendentals=0),
        name=body.__name__,
    )(*args)


def send(value, to):
    nx, ny = lax.axis_size("gx"), lax.axis_size("gy")
    pairs = []
    for i in range(nx):
        for j in range(ny):
            goal = to(i, j)
            if goal is not None and 0 <= goal[0] < nx and 0 <= goal[1] < ny:
                pairs.append((i * ny + j, goal[0] * ny + goal[1]))
    return lax.ppermute(value, ("gx", "gy"), pairs)


def after(value, *others):
    return lax.optimization_barrier((value, *others))[0]


def over_core(value):
    return send(value, lambda i, j: (i ^ 1, j))


def over_x(value):
    return send(value, lambda i, j: (i, j ^ 1))


def over_z(value):
    return send(value, lambda i, j: (i ^ 2, j))


def over_xz(value):
    return send(value, lambda i, j: (i ^ 2, j ^ 1))


def over_x_or_z(value):
    return send(value, lambda i, j: (i ^ 2, j) if i % 2 else (i, j ^ 1))


def over_edge(value):
    nx, ny = lax.axis_size("gx"), lax.axis_size("gy")

    def to(i, j):
        if i % 2 == 0:
            return ((i + 2) % nx if (i // 2) % 2 else (i - 2) % nx, j)
        return (i, (j + 1) % ny if j % 2 else (j - 1) % ny)

    return send(value, to)


def local(leaf_map, source_trace, tile_class, absorb_table):
    H = S // 2
    leaf = leaf_map[0, 0]
    oth = over_core(leaf)
    classes = tile_class[0, 0]
    chosen = (classes[:, None] == jnp.arange(absorb_table.shape[0], dtype=jnp.int32)[None, :]).astype(f32)
    levels = jnp.sum(chosen * absorb_table[None, :], axis=1)
    seg = leaf.shape[0] // classes.shape[0]
    spread = jnp.broadcast_to(levels[:, None], (classes.shape[0], seg)).reshape(-1)
    hown = (spread * source_trace[0, 0])[None]
    hoth = over_core(hown)
    (mark,) = call(bring, [(8, S)], [], [leaf], 1.0)
    minv1, pii, xi = call(
        level1_interface, [(S, S), (2 * S, 2 * S), (S + 8, 2 * S)], [], [leaf, oth, hown, hoth, mark], 2.5
    )
    xin = over_x(xi)
    m1, xe, xl = call(
        level1_map, [(6 * S, 7 * S), (S, 4 * S), (H, 5 * S)], [], [leaf, oth, hown, hoth, minv1], 2.0
    )
    xen = over_x(xe)
    xic = over_core(after(xin, xe))
    minv, gii = call(level2_inverse, [(2 * S, 2 * S)] * 2, [(2 * S, 2 * S)], [pii, xin, xic], 0.5)
    xec = over_core(after(xen, minv))
    xln = over_x(after(xl, xen, minv))
    yi, yh, yd = call(
        level2_interface,
        [(S + 8, 2 * S), (H + 8, 2 * S), (S, S)],
        [(2 * S, 2 * S)],
        [minv, gii, m1, xin, xic, xen, xec],
        1.0,
    )
    a1, a2 = over_x_or_z(yi), over_xz(yh)
    t, ye, chip, rr = call(
        level2_rest,
        [(2 * S, 9 * S), (S, 6 * S), (3 * S, 3 * S), (H + 8, 6 * S)],
        [(2 * S, 5 * S)],
        [after(minv, yd), gii, m1, xin, xic, xen, xec],
        0.01,
    )
    be, yx = call(level2_edge, [(S, 6 * S), (H, 6 * S)], [], [t, m1, ye, xln], 0.01)
    a1, a2, _, chip = lax.optimization_barrier((a1, a2, be, chip))
    k1, k2 = over_core(a1), over_core(a2)
    bn = over_z(be)
    rn = over_x(after(rr, be))
    minv3, gii3, th, hs = call(
        level3_inverse,
        [(2 * S, 2 * S), (2 * S, 2 * S), (2 * S, S), (8, 2 * S)],
        [(2 * S, 2 * S)] * 3,
        [yi, yd, a1, k1, a2, k2, chip],
        0.3,
    )
    g0 = over_edge(hs)
    rc = over_core(after(rn, minv3))
    yk = over_core(after(yx, minv3))
    (rows,) = call(level2_rows, [(3 * H, 9 * S)], [(3 * H, 7 * S)], [t, m1, rn, after(rc, yk)], 1.5)
    bn, g0, rows = lax.optimization_barrier((bn, g0, rows))
    kb = over_core(bn)
    gx, gz, gd = over_x(g0), over_z(g0), over_xz(g0)
    top, raw, h3 = call(
        level3_rows,
        [(3 * H, 12 * S), (3 * H, 12 * S), (3 * H, S)],
        [(2 * S, 6 * S)] * 2,
        [minv3, gii3, th, ye, yx, yk, bn, kb, rows],
        2.5,
    )
    g0, gx, gz, gd, h3 = lax.optimization_barrier((g0, gx, gz, gd, h3))
    edges = jnp.concatenate([g0, gx, gz, gd], 0)
    (out,) = call(couple, [(1, 3 * H)], [(8, 12 * S)], [raw, h3, edges, over_core(edges)], 0.7)
    return top[None, None], out[None]


def solution(mesh):
    return jax.shard_map(
        local,
        mesh=mesh,
        in_specs=(P("gx", "gy", None, None), P("gx", "gy", None), P("gx", "gy", None), P()),
        out_specs=(P("gx", "gy", None, None), P("gx", "gy", None)),
        check_vma=False,
    )
```

```python
import math

import jax
import jax.numpy as jnp
from jax import lax
from jax.experimental import pallas as pl
from jax.experimental.pallas import tpu as pltpu
from jax.sharding import PartitionSpec as P

S = 128
f32 = jnp.float32
bf16 = jnp.bfloat16
HIGHEST = lax.Precision.HIGHEST


def roles():
    gx = lax.axis_index("gx")
    gy = lax.axis_index("gy")
    return gx % 2, gy % 2, (gx // 2) % 2


def at(offset, size, unit=S):
    return pl.ds(pl.multiple_of(offset * unit, unit), size)


def split(x):
    high = x.astype(bf16)
    return high, (x - high.astype(f32)).astype(bf16)


def mm(a, b):
    return jnp.dot(a, b, preferred_element_type=f32)


def dot3s(a, b):
    return mm(a[0], b[0]) + (mm(a[0], b[1]) + mm(a[1], b[0]))


def dot3(a, b):
    return dot3s(split(a), split(b))


def dot_full(a, b):
    return jnp.dot(a, b, precision=HIGHEST, preferred_element_type=f32)


def inverse(K):
    n = K.shape[0]
    rows = lax.broadcasted_iota(jnp.int32, (n, n), 0)
    cols = lax.broadcasted_iota(jnp.int32, (n, n), 1)
    eye = (rows == cols).astype(f32)
    ks = split(K)
    X = eye + K
    power = mm(ks[0], ks[0])
    steps = 6
    for j in range(1, steps + 1):
        pb = power.astype(bf16)
        if j < steps:
            both = mm(jnp.concatenate([X.astype(bf16), pb], 0), pb)
            X = X + both[:n]
            power = both[n:]
        else:
            X = X + mm(X.astype(bf16), pb)
    xs = split(X)
    residual = eye - X + dot3s(ks, xs)
    X = X + mm(xs[0], residual.astype(bf16))
    residual = eye - X + dot_full(K, X)
    return X + dot3(X, residual)


def as_columns(row):
    return jnp.broadcast_to(row, (S, S)).T


def as_rows(block):
    return block.T[:8]


def bring(leaf, mark):
    mark[...] = leaf[:8, :S]


def level1_interface(own, oth, hown, hoth, mark, minv, pii, xi):
    c, s, r = roles()
    d = 1 - c
    e = 3 - s
    P_ii = own[at(d, S), at(d, S)]
    Q_ii = split(oth[at(c, S), at(c, S)])
    P_ie = own[at(d, S), at(e, S)]
    Q_ie = oth[at(c, S), at(e, S)]
    p_i = as_columns(hown[:, at(d, S)])
    q_i = as_columns(hoth[:, at(c, S)])
    X = inverse(dot_full(oth[at(c, S), at(c, S)], P_ii))
    minv[...] = X
    U = dot3s(Q_ii, split(jnp.concatenate([P_ie, p_i], 1)))
    T = split(dot3(X, jnp.concatenate([-U[:, :S], Q_ie, q_i - U[:, S:]], 1)))
    D = dot3s(split(own[at(e, S), at(d, S)]), T)
    Tp = jnp.concatenate([P_ie, jnp.zeros((S, S), f32)], 1) - dot3s(split(P_ii), (T[0][:, : 2 * S], T[1][:, : 2 * S]))
    DQ = dot3(oth[at(e, S), at(c, S)], Tp)
    pii[at(c, S), at(c, S)] = own[at(e, S), at(e, S)] - D[:, :S]
    pii[at(c, S), at(d, S)] = -D[:, S : 2 * S]
    pii[at(d, S), at(c, S)] = -DQ[:, :S]
    pii[at(d, S), at(d, S)] = oth[at(e, S), at(e, S)] - DQ[:, S:]
    xi[:S] = pii[at(c, S), :]
    xi[S:, :S] = as_rows(as_columns(hown[:, at(e, S)]) - D[:, 2 * S :])
    xi[S:, S:] = jnp.zeros((8, S), f32)


def level1_map(own, oth, hown, hoth, minv, m1, xe, xl):
    c, s, r = roles()
    d = 1 - c
    P_ii = own[at(d, S), at(d, S)]
    Q_ii = oth[at(c, S), at(c, S)]
    P_ie = jnp.concatenate([own[at(d, S), at(c, S)], own[at(d, S), 2 * S :]], 1)
    Q_ie = jnp.concatenate([oth[at(c, S), at(d, S)], oth[at(c, S), 2 * S :]], 1)
    p_i = as_columns(hown[:, at(d, S)])
    q_i = as_columns(hoth[:, at(c, S)])
    U = dot3(Q_ii, jnp.concatenate([P_ie, p_i], 1))
    Z = jnp.concatenate([-U[:, : 3 * S], Q_ie, q_i - U[:, 3 * S :]], 1)
    T = dot3(minv[...], Z)
    ts = split(T)
    Tp = jnp.concatenate([P_ie, jnp.zeros((S, 3 * S), f32), p_i], 1) - dot3s(split(P_ii), ts)
    P_ei = jnp.concatenate([own[at(c, S), at(d, S)], own[2 * S :, at(d, S)]], 0)
    Q_ei = jnp.concatenate([oth[at(d, S), at(c, S)], oth[2 * S :, at(c, S)]], 0)
    DP = dot3s(split(P_ei), ts)
    DQ = dot3(Q_ei, Tp)
    for k in range(3):
        mine = slice(k * S, (k + 1) * S)
        row_own = at(c, S) if k == 0 else slice((k + 1) * S, (k + 2) * S)
        row_oth = at(d, S) if k == 0 else slice((k + 1) * S, (k + 2) * S)
        to_own = at(c + 2 * k, S)
        to_oth = at(d + 2 * k, S)
        for n in range(3):
            col_own = at(c, S) if n == 0 else slice((n + 1) * S, (n + 2) * S)
            col_oth = at(d, S) if n == 0 else slice((n + 1) * S, (n + 2) * S)
            n_own = slice(n * S, (n + 1) * S)
            n_oth = slice((n + 3) * S, (n + 4) * S)
            m1[to_own, at(c + 2 * n, S)] = own[row_own, col_own] - DP[mine, n_own]
            m1[to_own, at(d + 2 * n, S)] = -DP[mine, n_oth]
            m1[to_oth, at(d + 2 * n, S)] = oth[row_oth, col_oth] - DQ[mine, n_oth]
            m1[to_oth, at(c + 2 * n, S)] = -DQ[mine, n_own]
        h_own = hown[:, at(c, S)] if k == 0 else hown[:, (k + 1) * S : (k + 2) * S]
        h_oth = hoth[:, at(d, S)] if k == 0 else hoth[:, (k + 1) * S : (k + 2) * S]
        m1[to_own, 6 * S :] = as_columns(h_own) - DP[mine, 6 * S :]
        m1[to_oth, 6 * S :] = as_columns(h_oth) - DQ[mine, 6 * S :]
    row = at(2 * (2 - s) + c, S)
    xe[:, : 2 * S] = m1[row, : 2 * S]
    xe[:, 2 * S :] = m1[row, at(2 * (1 + s), 2 * S)]
    half = at(2 * (1 - r) + c, S // 2, S // 2)
    xl[:, :S] = m1[half, at(r, S)]
    xl[:, S:] = m1[half, 2 * S : 6 * S]


def pick(x, s, low, high):
    return jnp.where(s == 0, x[:, 2 * S * low : 2 * S * (low + 1)], x[:, 2 * S * high : 2 * S * (high + 1)])


def level2_inverse(pii, xin, xic, minv, gii, qii):
    c, s, r = roles()
    qii[at(c, S), :] = xin[:S]
    qii[at(1 - c, S), :] = xic[:S]
    X = inverse(dot_full(qii[...], pii[...]))
    minv[...] = X
    gii[...] = dot3(X, qii[...])


def level2_interface(minv, gii, m1, xin, xic, xen, xec, yi, yh, yd, qe):
    c, s, r = roles()
    d = 1 - c
    H = S // 2
    inner = at(2 * (2 - s), 2 * S)
    side = at(1 - r, S)
    A = dot3(gii[...], jnp.concatenate([m1[inner, side], m1[inner, 6 * S :]], 1))
    qe[at(c, S), :S] = xen[:, side]
    qe[at(d, S), :S] = xec[:, side]
    qe[at(c, S), S:] = as_columns(xin[S : S + 1, :S])
    qe[at(d, S), S:] = as_columns(xic[S : S + 1, :S])
    B = dot3(minv[...], qe[...])
    D = dot3(m1[side, inner], jnp.concatenate([A[:, :S], B[:, :S], B[:, S:] - A[:, S:]], 1))
    data = m1[side, 6 * S :] - D[:, 2 * S :]
    yd[...] = data
    yi[:S, at(s, S)] = m1[side, side] + D[:, :S]
    yi[:S, at(1 - s, S)] = -D[:, S : 2 * S]
    yi[S:, :S] = as_rows(data)
    yi[S:, S:] = jnp.zeros((8, S), f32)
    yh[:H] = yi[at(c, H, H), :]
    yh[H:] = yi[S:]


def level2_rest(minv, gii, m1, xin, xic, xen, xec, t, ye, chip, rr, qe):
    c, s, r = roles()
    o = 1 - s
    H = S // 2
    inner = at(2 * (2 - s), 2 * S)
    outer = at(2 * (1 + s), 2 * S)
    P_e = jnp.concatenate([m1[inner, : 2 * S], m1[inner, outer], m1[inner, 6 * S :]], 1)
    A = dot3(gii[...], P_e)
    qe[at(c, S), : 4 * S] = xen[...]
    qe[at(1 - c, S), : 4 * S] = xec[...]
    qe[at(c, S), 4 * S :] = as_columns(xin[S : S + 1, :S])
    qe[at(1 - c, S), 4 * S :] = as_columns(xic[S : S + 1, :S])
    B = dot3(minv[...], qe[...])
    t[:, at(s, S)] = -A[:, :S]
    t[:, at(2 + s, S)] = -A[:, S : 2 * S]
    t[:, at(4 + 2 * s, 2 * S)] = -A[:, 2 * S : 4 * S]
    t[:, at(o, S)] = B[:, :S]
    t[:, at(2 + o, S)] = B[:, S : 2 * S]
    t[:, at(4 + 2 * o, 2 * S)] = B[:, 2 * S : 4 * S]
    t[:, 8 * S :] = B[:, 4 * S :] - A[:, 4 * S :]
    row = at(1 - r, S)
    ye[...] = -dot3(m1[row, inner], jnp.concatenate([t[:, at(2 * r, 2 * S)], t[:, 4 * S : 8 * S]], 1))
    ye[:, at(s, S)] += m1[row, at(r, S)]
    ye[:, at(2 + 2 * s, 2 * S)] += m1[row, outer]
    P_ei = jnp.concatenate([m1[at(r, S), inner], m1[outer, inner]], 0)
    T_i = jnp.concatenate([t[:, at(2 * (1 - r), 2 * S)], t[:, 8 * S :]], 1)
    chip[...] = -dot3(P_ei, T_i)
    chip[:S, at(s, S)] += m1[at(r, S), at(1 - r, S)]
    chip[S:, at(s, S)] += m1[outer, at(1 - r, S)]
    chip[:S, 2 * S :] += m1[at(r, S), 6 * S :]
    chip[S:, 2 * S :] += m1[outer, 6 * S :]
    first = jnp.where(c == 0, jnp.where(s == 0, 4, 2 * r), jnp.where(s == 0, 5, 8))
    lines = at(first, H, H)
    rr[:H] = m1[lines, : 6 * S]
    rr[H:, :S] = as_rows(jnp.concatenate([m1[lines, 6 * S :]] * 2, 0))
    rr[H:, S:] = jnp.zeros((8, 5 * S), f32)


def level2_edge(t, m1, ye, xln, be, yx):
    c, s, r = roles()
    o = 1 - s
    H = S // 2
    inner = at(2 * (2 - s), 2 * S)
    link = pick(xln[:, S:], s, 0, 1)
    V = dot3(link, m1[inner, : 6 * S])
    D = dot3(pick(V, s, 2, 1), jnp.concatenate([t[:, at(2 * r, 2 * S)], t[:, 4 * S : 8 * S]], 1))
    yx[...] = D
    yx[:, at(s, S)] -= jnp.where(r == 0, V[:, :S], V[:, S : 2 * S])
    yx[:, at(2 + 2 * s, 2 * S)] -= pick(V, s, 1, 2)
    yx[:, at(o, S)] += xln[:, :S]
    yx[:, at(2 + 2 * o, 2 * S)] += pick(xln[:, S:], s, 1, 0)
    be[:H] = ye[at(c, H, H), :]
    be[H:] = yx[...]


def level2_rows(t, m1, rn, rc, rows, work):
    c, s, r = roles()
    o = 1 - s
    H = S // 2
    inner = at(2 * (2 - s), 2 * S)
    outer = at(2 * (1 + s), 2 * S)
    m = 2 * c + s

    @pl.when(m == 0)
    def _():
        work[: 2 * H] = m1[at(2 * r, 2 * H, H), :]

    @pl.when(m == 1)
    def _():
        work[:H] = m1[at(2 * r + 1, H, H), :]
        work[H : 2 * H, : 6 * S] = rn[:H]
        work[H : 2 * H, 6 * S :] = as_columns(rn[H : H + 1, :S])[:H]
        work[2 * H :, : 6 * S] = rc[:H]
        work[2 * H :, 6 * S :] = as_columns(rc[H : H + 1, :S])[:H]

    @pl.when(m == 2)
    def _():
        work[: 2 * H] = m1[6 * H : 8 * H, :]

    @pl.when((m == 0) | (m == 2))
    def _():
        work[2 * H :, : 6 * S] = rn[:H]
        work[2 * H :, 6 * S :] = as_columns(rn[H : H + 1, :S])[:H]

    @pl.when(m == 3)
    def _():
        work[...] = m1[9 * H : 12 * H, :]

    start = jnp.where(m == 1, H, jnp.where(m == 3, 3 * H, 2 * H))
    index = lax.broadcasted_iota(jnp.int32, (3 * H, 1), 0)
    got = index >= start
    V = dot3(work[:, outer], m1[inner, :])
    rows[:, : 7 * S] = V
    V_ii = rows[:, inner]
    V_pair = rows[:, outer]
    C = jnp.where(got, V_ii, -work[:, inner])
    D = dot3(C, t[...])
    own_side = jnp.where(got, -V[:, : 2 * S], work[:, : 2 * S])
    own_pair = jnp.where(got, -V_pair, work[:, outer])
    oth_side = jnp.where(got, work[:, : 2 * S], 0.0)
    oth_pair = jnp.where(got, work[:, inner], 0.0)
    data = work[:, 6 * S :] - jnp.where(got, V[:, 6 * S :], 0.0)
    rows[...] = D
    rows[:, at(s, S)] += own_side[:, :S]
    rows[:, at(2 + s, S)] += own_side[:, S:]
    rows[:, at(4 + 2 * s, 2 * S)] += own_pair
    rows[:, at(o, S)] += oth_side[:, :S]
    rows[:, at(2 + o, S)] += oth_side[:, S:]
    rows[:, at(4 + 2 * o, 2 * S)] += oth_pair
    rows[:, 8 * S :] += data


def level3_inverse(yi, yd, a1, k1, a2, k2, chip, minv, gii, th, hs, pii, qii, pq):
    c, s, r = roles()
    o = 1 - s
    d = 1 - c
    H = S // 2
    x = jnp.where(c == 0, a1[...], k1[...])
    z = jnp.where(c == 0, k1[...], a1[...])
    pii[at(s, S), :] = yi[:S]
    pii[at(o, S), :] = x[:S]
    qii[at(s, S), :] = z[:S]
    qii[at(2 * o + c, H, H), :] = a2[:H]
    qii[at(2 * o + d, H, H), :] = k2[:H]
    pq[at(s, S), :S] = yd[...]
    pq[at(o, S), :S] = as_columns(x[S : S + 1, :S])
    pq[at(s, S), S:] = as_columns(z[S : S + 1, :S])
    pq[at(o, S), S:] = as_columns(a2[H : H + 1, :S])
    X = inverse(dot_full(qii[...], pii[...]))
    xs = split(X)
    minv[...] = X
    G = dot3s(xs, split(qii[...]))
    gii[...] = G
    tv = dot3s(xs, split(pq[:, S:])) - dot3(G, pq[:, :S])
    th[...] = tv
    h3 = chip[:, 2 * S :] - dot3(chip[:, : 2 * S], tv)
    hs[:, :S] = jnp.where(c == 0, as_rows(h3[:S]), as_rows(h3[S : 2 * S]))
    hs[:, S:] = as_rows(h3[2 * S :])


def level3_rows(minv, gii, th, ye, yx, yk, be, kb, rows, top, raw, h3, pe, qe):
    c, s, r = roles()
    o = 1 - s
    d = 1 - c
    H = S // 2
    pe[at(s, S), :] = ye[...]
    pe[at(2 * o + c, H, H), :] = yx[...]
    pe[at(2 * o + d, H, H), :] = yk[...]
    qe[at(2 * s + c, H, H), :] = be[:H]
    qe[at(2 * s + d, H, H), :] = kb[:H]
    qe[at(2 * o + c, H, H), :] = be[H:]
    qe[at(2 * o + d, H, H), :] = kb[H:]
    A = dot3(gii[...], pe[...])
    B = dot3(minv[...], qe[...])
    R_ei = split(rows[:, at(2 * (1 - r), 2 * S)])
    scale = math.sqrt(12 * S)
    R_ee = jnp.concatenate([rows[:, at(2 * r, 2 * S)], rows[:, 4 * S : 8 * S]], 1)
    own = R_ee + dot3s(R_ei, split(A))
    oth = -dot3s(R_ei, split(B))
    raw[:, at(6 * r, 6 * S)] = own
    raw[:, at(6 * (1 - r), 6 * S)] = oth
    top[...] = raw[...] * scale
    h3[...] = rows[:, 8 * S :] - dot3s(R_ei, split(th[...]))


def couple(raw, h3, mine, core, out, inc):
    c, s, r = roles()
    box_x = lax.axis_index("gx") // 4
    box_y = lax.axis_index("gy") // 2
    last_x = lax.axis_size("gx") // 4 - 1
    last_y = lax.axis_size("gy") // 2 - 1
    edge_x = (box_x == 0) | (box_x == last_x)
    edge_y = (box_y == 0) | (box_y == last_y)
    at_x = jnp.where(box_x == 0, 0, 1)
    at_y = jnp.where(box_y == 0, 0, 1)
    for n, (ss, rr) in enumerate(((s, r), (1 - s, r), (s, 1 - r), (1 - s, 1 - r))):
        lines = slice(8 * n, 8 * n + 8)
        side = jnp.where(c == 0, mine[lines, :S], core[lines, :S])
        pair = jnp.where(c == 0, core[lines, :], mine[lines, :])
        inc[:, at(6 * rr + ss, S)] = jnp.where(edge_x & (at_x == rr), 0.0, side)
        inc[:, at(6 * rr + 2 + 2 * ss, 2 * S)] = jnp.where(edge_y & (at_y == ss), 0.0, pair)
    lane = lax.broadcasted_iota(jnp.int32, (h3.shape[0], S), 1)
    total = jnp.where(lane == 0, h3[...], 0.0)
    for k in range(12):
        total = total - raw[:, k * S : (k + 1) * S] * inc[0:1, k * S : (k + 1) * S]
    lines = jnp.concatenate([total, jnp.zeros((2 * S - h3.shape[0], S), f32)], 0)
    flat = jnp.concatenate([lines[:S].T, lines[S:].T], 1)
    out[...] = jnp.sum(flat, 0, keepdims=True)[:, : h3.shape[0]]


def call(body, outs, scratch, args, us):
    whole = pl.BlockSpec(memory_space=pltpu.VMEM)
    return pl.pallas_call(
        body,
        out_shape=[jax.ShapeDtypeStruct(o, f32) for o in outs],
        in_specs=[whole] * len(args),
        out_specs=[whole] * len(outs),
        scratch_shapes=[pltpu.VMEM(x, f32) for x in scratch],
        compiler_params=pltpu.CompilerParams(vmem_limit_bytes=24 * 1024 * 1024),
        cost_estimate=pl.CostEstimate(flops=int(us * 1.15e9), bytes_accessed=0, transcendentals=0),
        name=body.__name__,
    )(*args)


def send(value, to):
    nx, ny = lax.axis_size("gx"), lax.axis_size("gy")
    pairs = []
    for i in range(nx):
        for j in range(ny):
            goal = to(i, j)
            if goal is not None and 0 <= goal[0] < nx and 0 <= goal[1] < ny:
                pairs.append((i * ny + j, goal[0] * ny + goal[1]))
    return lax.ppermute(value, ("gx", "gy"), pairs)


def after(value, *others):
    return lax.optimization_barrier((value, *others))[0]


def over_core(value):
    return send(value, lambda i, j: (i ^ 1, j))


def over_x(value):
    return send(value, lambda i, j: (i, j ^ 1))


def over_z(value):
    return send(value, lambda i, j: (i ^ 2, j))


def over_xz(value):
    return send(value, lambda i, j: (i ^ 2, j ^ 1))


def over_x_or_z(value):
    return send(value, lambda i, j: (i ^ 2, j) if i % 2 else (i, j ^ 1))


def over_edge(value):
    nx, ny = lax.axis_size("gx"), lax.axis_size("gy")

    def to(i, j):
        if i % 2 == 0:
            return ((i + 2) % nx if (i // 2) % 2 else (i - 2) % nx, j)
        return (i, (j + 1) % ny if j % 2 else (j - 1) % ny)

    return send(value, to)


def local(leaf_map, source_trace, tile_class, absorb_table):
    H = S // 2
    leaf = leaf_map[0, 0]
    oth = over_core(leaf)
    classes = tile_class[0, 0]
    chosen = (classes[:, None] == jnp.arange(absorb_table.shape[0], dtype=jnp.int32)[None, :]).astype(f32)
    levels = jnp.sum(chosen * absorb_table[None, :], axis=1)
    seg = leaf.shape[0] // classes.shape[0]
    spread = jnp.broadcast_to(levels[:, None], (classes.shape[0], seg)).reshape(-1)
    hown = (spread * source_trace[0, 0])[None]
    hoth = over_core(hown)
    (mark,) = call(bring, [(8, S)], [], [leaf], 1.0)
    minv1, pii, xi = call(
        level1_interface, [(S, S), (2 * S, 2 * S), (S + 8, 2 * S)], [], [leaf, oth, hown, hoth, mark], 2.5
    )
    xin = over_x(xi)
    m1, xe, xl = call(
        level1_map, [(6 * S, 7 * S), (S, 4 * S), (H, 5 * S)], [], [leaf, oth, hown, hoth, minv1], 2.0
    )
    xen = over_x(xe)
    xic = over_core(after(xin, xe))
    minv, gii = call(level2_inverse, [(2 * S, 2 * S)] * 2, [(2 * S, 2 * S)], [pii, xin, xic], 0.5)
    xec = over_core(after(xen, minv))
    xln = over_x(after(xl, xen, minv))
    yi, yh, yd = call(
        level2_interface,
        [(S + 8, 2 * S), (H + 8, 2 * S), (S, S)],
        [(2 * S, 2 * S)],
        [minv, gii, m1, xin, xic, xen, xec],
        1.0,
    )
    a1, a2 = over_x_or_z(yi), over_xz(yh)
    t, ye, chip, rr = call(
        level2_rest,
        [(2 * S, 9 * S), (S, 6 * S), (3 * S, 3 * S), (H + 8, 6 * S)],
        [(2 * S, 5 * S)],
        [after(minv, yd), gii, m1, xin, xic, xen, xec],
        0.01,
    )
    be, yx = call(level2_edge, [(S, 6 * S), (H, 6 * S)], [], [t, m1, ye, xln], 0.01)
    a1, a2, _, chip = lax.optimization_barrier((a1, a2, be, chip))
    k1, k2 = over_core(a1), over_core(a2)
    bn = over_z(be)
    rn = over_x(after(rr, xln))
    minv3, gii3, th, hs = call(
        level3_inverse,
        [(2 * S, 2 * S), (2 * S, 2 * S), (2 * S, S), (8, 2 * S)],
        [(2 * S, 2 * S)] * 3,
        [yi, yd, a1, k1, a2, k2, chip],
        0.3,
    )
    g0 = over_edge(hs)
    rc = over_core(after(rn, minv3))
    yk = over_core(after(yx, minv3))
    (rows,) = call(level2_rows, [(3 * H, 9 * S)], [(3 * H, 7 * S)], [t, m1, rn, after(rc, yk)], 1.5)
    bn, g0, rows = lax.optimization_barrier((bn, g0, rows))
    kb = over_core(bn)
    gx, gz, gd = over_x(g0), over_z(g0), over_xz(g0)
    top, raw, h3 = call(
        level3_rows,
        [(3 * H, 12 * S), (3 * H, 12 * S), (3 * H, S)],
        [(2 * S, 6 * S)] * 2,
        [minv3, gii3, th, ye, yx, yk, bn, kb, rows],
        2.5,
    )
    g0, gx, gz, gd, h3 = lax.optimization_barrier((g0, gx, gz, gd, h3))
    edges = jnp.concatenate([g0, gx, gz, gd], 0)
    (out,) = call(couple, [(1, 3 * H)], [(8, 12 * S)], [raw, h3, edges, over_core(edges)], 0.7)
    return top[None, None], out[None]


def solution(mesh):
    return jax.shard_map(
        local,
        mesh=mesh,
        in_specs=(P("gx", "gy", None, None), P("gx", "gy", None), P("gx", "gy", None), P()),
        out_specs=(P("gx", "gy", None, None), P("gx", "gy", None)),
        check_vma=False,
    )
```
